32 devices in a mesh: groups: 2 (over y), pool: 4 (over z), tensor: 4 (over x, core).
Axes of the slice: x: 2, y: 2, z: 4, core: 2. Of those that a mesh axis runs over, the one named last changes fastest.
Arguments:
- hidden: bfloat16 [128, 2, 8192], P(('groups', 'pool')), parts along dimension 0, may hold values from -6 to 6
- queries: bfloat16 [128, 2, 64, 128], P(('groups', 'pool'), None, 'tensor'), parts along dimension 0, may hold values from -110 to 110
- cache: bfloat16 [128, 256, 8, 256], P(('groups', 'pool'), None, 'tensor'), parts along dimension 0, may hold values from -4 to 4
- key_value_weight: bfloat16 [8192, 8, 256], P('pool', 'tensor'), may hold values from -0.0625 to 0.0625
- adapter_down_weight: bfloat16 [24, 8192, 128], P('tensor', 'pool'), may hold values from -0.0625 to 0.0625
- adapter_up_key: bfloat16 [24, 64, 8, 128], P('pool', None, 'tensor'), may hold values from -0.75 to 0.75
- adapter_up_value: bfloat16 [24, 64, 8, 128], P('pool', None, 'tensor'), may hold values from -0.75 to 0.75
- request_adapter: int32 [128], P(('groups', 'pool')), parts along dimension 0, may hold values from 0 to 23
- adapter_storage: int32 [24], replicated, may hold values from 0 to 23, each once
- lengths: int32 [128], P(('groups', 'pool')), parts along dimension 0, may hold values from 1 to 256, 10240 in all
Outputs:
- attended: bfloat16 [128, 2, 8192], P(('groups', 'pool'), None, 'tensor'), parts along dimension 0
- fresh_key_value: bfloat16 [128, 2, 8, 256], P(('groups', 'pool'), None, 'tensor'), parts along dimension 0
The draws below stay inside these ranges and needn't reach their ends.
There are 2 independent parts, one for each index of `groups`. The reference program is written for one: setup_inputs(seed, part) draws one part's arguments, and reference() takes and returns one part's arrays. A program takes and returns all parts, laid end to end along the dimension named above; an argument that names none is the same for every part. Nothing has to cross between parts.
Inputs may be any that keep to these rules, and one draw needn't show every extreme that they name: `adapter_storage`: each slot from 0 to 23 holds exactly one adapter.
All inputs are finite; a program needn't handle non-finite values. No bound on the sum of `lengths` on one device may be relied on, other than what follows from the above.
Results may differ from the reference program's by a relative error of at most 0.0052.
Values may be sent and summed in bfloat16 or wider, within the bound.
No kernel may reach another device: no remote copies, remote signals or barrier semaphores. Data moves between devices by JAX's collectives and lax.ppermute only.
A program may use at most 64 MiB of HBM per device.

```python
import math
import jax
import jax.numpy as jnp
import numpy as np
from jax import lax

MODEL_WIDTH = 8192
HEADS = 64
KEY_VALUE_HEADS = 8
HEAD_SIZE = 128
ADAPTER_RANK = 64
NEW = 2
CACHE = 256
ROWS = 64
ADAPTER_POOL = 24


def shared_keys(key):
    return jax.random.truncated_normal(key, -4.0, 4.0, (ROWS, CACHE, KEY_VALUE_HEADS, HEAD_SIZE), jnp.float32)


def draw_cache(key, part):
    keys = shared_keys(key)
    key = jax.random.fold_in(key, 3)
    values = jax.random.truncated_normal(key, -4.0, 4.0, (ROWS, CACHE, KEY_VALUE_HEADS, HEAD_SIZE), jnp.float32)
    return jnp.concatenate([keys, values], axis=-1).astype(jnp.bfloat16)


def draw_queries(key, part):
    key = jax.random.fold_in(key, 5)
    drawn = jax.random.truncated_normal(key, -4.0, 4.0, (ROWS, NEW, HEADS, HEAD_SIZE), jnp.float32)
    return drawn.astype(jnp.bfloat16)


def with_ends(values, stream_key, low, top_value):
    index_at = [jax.random.randint(jax.random.fold_in(stream_key, axis), (), 0, length) for axis, length in enumerate(values.shape)]
    main_axis = values.shape.index(max(values.shape))
    neighbour = index_at[:main_axis] + [(index_at[main_axis] + 1) % values.shape[main_axis]] + index_at[main_axis + 1:]
    return values.at[tuple(index_at)].set(low).at[tuple(neighbour)].set(top_value)


def block_scale(own_key, extent, cuts, smallest, high):
    loudness = 1.0
    for dim, blocks in cuts:
        heights = jax.random.uniform(jax.random.fold_in(jax.random.fold_in(own_key, 6), dim), (blocks,), jnp.float32, smallest / len(cuts), high / len(cuts))
        loudness = loudness * jnp.repeat(jnp.exp(heights), extent[dim] // blocks).reshape((-1,) + (1,) * (len(extent) - 1 - dim))
    return loudness


def rank_table(count, skew):
    loads = [(1 << 20) // math.isqrt(standing ** skew) + 1 for standing in range(1, count + 1)]
    scale = 1 + sum(loads) // (1 << 30)
    return np.cumsum(np.array([max(1, weight // scale) for weight in loads]))


def skewed_ids(own_key, dims, number_of, skew):
    listing = rank_table(number_of, skew)
    pick = jax.random.randint(jax.random.fold_in(own_key, 1), dims, 0, int(listing[number_of - 1]))
    standing = jnp.searchsorted(jnp.asarray(listing, jnp.int32), pick, side="right")
    return jax.random.permutation(jax.random.fold_in(own_key, 2), number_of)[standing].astype(jnp.int32)


def split_up(count, total, bound, slope):
    weights = [(1 << 20) // math.isqrt(standing ** slope) + 1 for standing in range(2, count + 1)]
    spare, given = total - bound - (count - 1), [1] * (count - 1)
    while spare > 0:
        candidates = [i for i in range(count - 1) if given[i] < bound]
        whole, budget = sum([weights[i] for i in candidates]), spare
        for i in candidates:
            addition = min(bound - given[i], max(1, budget * weights[i] // whole), spare)
            given[i] = given[i] + addition
            spare = spare - addition
    return np.array([bound] + given)


def uneven(rng, count, total, reach, lean):
    if count == 2:
        one = jax.random.randint(rng, (), max(1, total - reach), min(reach, total - 1) + 1)
        return jnp.stack([one, total - one])
    sizes = jnp.asarray(split_up(count, total, reach, lean), jnp.int32)
    couples = (count - 1) // 2
    giver, taker = sizes[1:1 + 2 * couples:2], sizes[2:2 + 2 * couples:2]
    slack = jnp.minimum(giver - 1, reach - taker)
    moved = jax.random.randint(jax.random.fold_in(rng, 1), (couples,), 0, 1 << 20) % (slack + 1)
    sizes = sizes.at[1:1 + 2 * couples:2].set(giver - moved).at[2:2 + 2 * couples:2].set(taker + moved)
    return sizes[jax.random.permutation(jax.random.fold_in(rng, 2), count)]


def gaussian(own_key, dims, scale, reach, pieces=(), kind=jnp.bfloat16):
    gain = block_scale(own_key, dims, pieces, -0.22, 0.18) if pieces else 1.0
    array = jax.random.normal(own_key, dims, jnp.float32) * scale * gain
    return jnp.minimum(jnp.maximum(array, -reach), reach).astype(kind)


def setup_inputs(seed: int = 0, part: int = 0) -> dict:
    key_of = jax.random.split(jax.random.key(seed), 11)
    part_keys = jax.random.split(jax.random.fold_in(key_of[10], part), 11)
    hidden = gaussian(part_keys[0], (ROWS, NEW, MODEL_WIDTH), 1.0, 6.0, ((0, 4),))
    queries = draw_queries(jax.random.fold_in(jax.random.fold_in(key_of[10], part), 71), part)
    cache = draw_cache(jax.random.fold_in(jax.random.fold_in(key_of[10], part), 71), part)
    key_value_weight = gaussian(key_of[3], (MODEL_WIDTH, KEY_VALUE_HEADS, 2 * HEAD_SIZE), MODEL_WIDTH ** -0.5, 0.0625, ((0, 4), (1, 4)))
    adapter_down_weight = gaussian(key_of[4], (ADAPTER_POOL, MODEL_WIDTH, 2 * ADAPTER_RANK), MODEL_WIDTH ** -0.5, 0.0625, ((0, 4), (1, 4)))
    adapter_up_key = gaussian(key_of[5], (ADAPTER_POOL, ADAPTER_RANK, KEY_VALUE_HEADS, HEAD_SIZE), ADAPTER_RANK ** -0.5, 0.75, ((0, 4), (2, 4)))
    adapter_up_value = gaussian(key_of[6], (ADAPTER_POOL, ADAPTER_RANK, KEY_VALUE_HEADS, HEAD_SIZE), ADAPTER_RANK ** -0.5, 0.75, ((0, 4), (2, 4)))
    request_adapter = with_ends(skewed_ids(part_keys[7], (ROWS,), ADAPTER_POOL, 2), jax.random.fold_in(part_keys[7], 3), 0, ADAPTER_POOL - 1).astype(jnp.int32)
    adapter_storage = jax.random.permutation(key_of[8], ADAPTER_POOL).astype(jnp.int32)
    lengths = uneven(part_keys[9], ROWS, ROWS * CACHE * 5 // 8, CACHE, 2).astype(jnp.int32)
    return {"hidden": hidden, "queries": queries, "cache": cache, "key_value_weight": key_value_weight, "adapter_down_weight": adapter_down_weight, "adapter_up_key": adapter_up_key, "adapter_up_value": adapter_up_value, "request_adapter": request_adapter, "adapter_storage": adapter_storage, "lengths": lengths}


ADAPTER_SCALE = 0.5


def attend(queries, cache, fresh_key_value, lengths):
    rows, steps_new, heads, head_dim = queries.shape
    kv_count = cache.shape[2]
    depth = cache.shape[1]
    group = heads // kv_count
    keys = jnp.concatenate([cache[..., :head_dim], fresh_key_value[..., :head_dim]], axis=1)
    values = jnp.concatenate([cache[..., head_dim:], fresh_key_value[..., head_dim:]], axis=1)
    grouped = queries.reshape(rows, steps_new, kv_count, group, head_dim)
    scores = jnp.einsum('rnkgd,rpkd->rnkgp', grouped.astype(jnp.float32), keys.astype(jnp.float32)) * (head_dim ** -0.5)
    places = jnp.arange(depth + steps_new, dtype=jnp.int32)
    turns = jnp.arange(steps_new, dtype=jnp.int32)
    valid = jnp.where(places[None, None, :] < depth, places[None, None, :] < lengths[:, None, None], (places[None, None, :] - depth) <= turns[None, :, None])
    scores = jnp.where(valid[:, :, None, None, :], scores, -1e30)
    weights = jax.nn.softmax(scores, axis=-1).astype(jnp.bfloat16)
    mixed = jnp.einsum('rnkgp,rpke->rnkge', weights.astype(jnp.float32), values.astype(jnp.float32))
    return mixed.reshape(rows, steps_new, heads * head_dim).astype(jnp.bfloat16)


def reference(hidden, queries, cache, key_value_weight, adapter_down_weight, adapter_up_key, adapter_up_value, request_adapter, adapter_storage, lengths):
    slots = adapter_storage[request_adapter].astype(jnp.int32)
    base_output = jnp.einsum('rnd,dke->rnke', hidden.astype(jnp.float32), key_value_weight.astype(jnp.float32))

    def shrink_row(item):
        row_states, storage_position = item
        down_matrix = lax.dynamic_index_in_dim(adapter_down_weight, storage_position, 0, keepdims=False)
        return jnp.dot(row_states, down_matrix, preferred_element_type=jnp.float32)

    reduced_input = lax.map(shrink_row, (hidden, slots)).astype(jnp.bfloat16)

    def expand_row(item):
        lowrank, storage_position = item
        key_up_matrix = lax.dynamic_index_in_dim(adapter_up_key, storage_position, 0, keepdims=False).astype(jnp.float32)
        value_up_matrix = lax.dynamic_index_in_dim(adapter_up_value, storage_position, 0, keepdims=False).astype(jnp.float32)
        widened = lowrank.astype(jnp.float32)
        delta_key = jnp.einsum('nr,rke->nke', widened[:, :ADAPTER_RANK], key_up_matrix)
        delta_value = jnp.einsum('nr,rke->nke', widened[:, ADAPTER_RANK:], value_up_matrix)
        return jnp.concatenate([delta_key, delta_value], axis=-1)

    adapter_update = lax.map(expand_row, (reduced_input, slots))
    fresh_key_value = (base_output + ADAPTER_SCALE * adapter_update).astype(jnp.bfloat16)

    def attend_row(item):
        query_row, cache_row, fresh_row, length_row = item
        return attend(query_row[None], cache_row[None], fresh_row[None], length_row[None])[0]

    attended = lax.map(attend_row, (queries, cache, fresh_key_value, lengths))
    return attended, fresh_key_value
```

```python
import functools
import jax
import jax.numpy as jnp
from jax import lax
from jax.experimental import pallas as pl
from jax.experimental.pallas import tpu as pltpu
from jax.sharding import PartitionSpec as P

ADAPTER_SCALE = 0.5
LANES = 128
F32 = jnp.float32
BF16 = jnp.bfloat16
VMEM = pl.BlockSpec(memory_space=pltpu.VMEM)
SMEM = pl.BlockSpec(memory_space=pltpu.SMEM)
HIGH = 100 * 1024 * 1024 // 2


def dot(a, b):
    return jnp.dot(a, b, preferred_element_type=F32)


def dot_t(a, b):
    return lax.dot_general(a, b, (((1,), (1,)), ((), ())), preferred_element_type=F32)


def struct(shape, dtype):
    return jax.ShapeDtypeStruct(shape, dtype)


def cost(flops, moved):
    return pl.CostEstimate(flops=int(flops), bytes_accessed=int(moved), transcendentals=0)


def pack_kernel(pool, parts, place, request_adapter, adapter_storage, hidden, *outs):
    rows, steps_new, width = hidden.shape
    count = rows * steps_new
    part = width // pool
    half = part // parts
    me, side = place[0], place[1]
    row = lax.broadcasted_iota(jnp.int32, (count, LANES), 0) // steps_new
    slots = jnp.zeros((count, LANES), jnp.int32)
    for r in range(rows):
        slots = jnp.where(row == r, adapter_storage[request_adapter[r]], slots)
    slots = slots.astype(F32).astype(BF16)
    for k in range(pool):
        start = (me ^ k) * part
        mine = pl.multiple_of(start + side * half, LANES)
        outs[k][:, :half] = hidden[:, :, pl.ds(mine, half)].reshape(count, half)
        outs[k][:, half:] = slots
    if parts == 2:
        other = pl.multiple_of(me * part + (1 - side) * half, LANES)
        outs[pool][...] = hidden[:, :, pl.ds(other, half)].reshape(count, half)


def project_kernel(pool, parts, place, *refs):
    chunks, refs = refs[:pool], refs[pool:]
    if parts == 2:
        own_other, swapped, refs = refs[0], refs[1:pool], refs[pool:]
    weight, down, base, slots_out, shrink = refs
    me, side, first_slot = place[0], place[1], place[2]
    count = chunks[0].shape[0]
    half = chunks[0].shape[1] - LANES
    kv_local = weight.shape[0]
    sides = [(side * half, jnp.concatenate([c[:, :half] for c in chunks], axis=0))]
    if parts == 2:
        rest = [own_other[...]] + [c[:, :half] for c in swapped]
        sides.append(((1 - side) * half, jnp.concatenate(rest, axis=0)))
    slots = jnp.concatenate([c[:, half:] for c in chunks], axis=0)
    slots_out[...] = slots
    slots = slots.astype(F32)
    step = 2 if down.shape[0] % 2 == 0 else 1
    total = jnp.zeros((count * pool, LANES), F32)
    for a in range(0, down.shape[0], step):
        out = 0.0
        for start, x in sides:
            at = pl.ds(pl.multiple_of(start, half), half)
            out += dot(x, jnp.concatenate([down[a + i, at, :] for i in range(step)], axis=1))
        for i in range(step):
            match = slots == (first_slot + a + i).astype(F32)
            total = jnp.where(match, out[:, i * LANES:(i + 1) * LANES], total)
    total = total.astype(BF16)
    for k in range(pool):
        at = pl.ds(pl.multiple_of((me ^ k) * count, count), count)
        shrink[at, :] = total[k * count:(k + 1) * count]
    for k in range(kv_local):
        out = 0.0
        for start, x in sides:
            at = pl.ds(pl.multiple_of(start, half), half)
            out += dot(x, weight[k, at, :])
        base[:, k * weight.shape[2]:(k + 1) * weight.shape[2]] = out


def expand_kernel(pool, parts, place, *refs):
    sums, refs = refs[:parts], refs[parts:]
    slots_in, base, up_key, up_value = refs[:4]
    outs, scratch = refs[4:4 + pool], refs[4 + pool]
    me, first_slot = place[0], place[3]
    holders, rank, kv_local, size = up_key.shape
    count = base.shape[0] // pool
    total = sums[0][...]
    for s in sums[1:]:
        total = total + s[...]
    scratch[...] = total
    ordered = jnp.concatenate(
        [scratch[pl.ds(pl.multiple_of((me ^ k) * count, count), count), :] for k in range(pool)], axis=0
    ).astype(BF16)
    slots = slots_in[...].astype(F32)
    deep = rank * kv_local
    for which, up in ((0, up_key), (1, up_value)):
        row = lax.broadcasted_iota(jnp.int32, (2 * rank, deep), 0)
        col = lax.broadcasted_iota(jnp.int32, (2 * rank, deep), 1)
        wide = []
        for k in range(kv_local):
            pick = (row == which * rank + col // kv_local) & (col % kv_local == k)
            wide.append(dot(ordered, pick.astype(F32).astype(BF16)))
        acc = [jnp.zeros((base.shape[0], size), F32) for _ in range(kv_local)]
        for a in range(holders):
            match = slots == (first_slot + a).astype(F32)
            if deep != LANES:
                match = match[:, :1]
            table = up[a].reshape(deep, size)
            for k in range(kv_local):
                acc[k] = acc[k] + dot(jnp.where(match, wide[k], 0.0).astype(BF16), table)
        for k in range(kv_local):
            at = slice((2 * k + which) * size, (2 * k + which + 1) * size)
            value = base[:, at] + ADAPTER_SCALE * acc[k]
            outs[0][:, at] = value[:count]
            for j in range(1, pool):
                outs[j][:, at] = value[j * count:(j + 1) * count].astype(BF16)


def cache_kernel(rows_step, lengths, queries, cache, acc_out, stat_out):
    _, steps_new, heads, size = queries.shape
    depth, kv_local = cache.shape[1], cache.shape[2]
    count = steps_new * heads
    group = heads // kv_local
    scale = size ** -0.5
    col = lax.broadcasted_iota(jnp.int32, (count, depth * kv_local), 1)
    row = lax.broadcasted_iota(jnp.int32, (count, depth * kv_local), 0)
    same = col % kv_local == row % heads // group
    lane = lax.broadcasted_iota(jnp.int32, (count, LANES), 1)
    for i in range(rows_step):
        r = pl.program_id(0) * rows_step + i
        q = queries[i].reshape(count, size)
        both = cache[i].reshape(depth * kv_local, 2 * size)
        scores = dot_t(q, both[:, :size]) * scale
        scores = jnp.where(same & (col < lengths[r] * kv_local), scores, -1e30)
        top = jnp.max(scores, axis=1, keepdims=True)
        weights = jnp.exp(scores - top)
        total = jnp.sum(weights, axis=1, keepdims=True)
        at = pl.ds(i * count, count)
        acc_out[at, :] = dot(weights.astype(BF16), both[:, size:])
        stat_out[at, :] = jnp.where(lane == 0, top, total)


def finish_kernel(pool, own, *refs):
    parts, refs = refs[:pool - 1], refs[pool - 1:]
    queries, acc_in, stat_in, attended, fresh_out, scratch = refs
    rows, steps_new, heads, size = queries.shape
    count = rows * steps_new
    kv_local = own.shape[1] // (2 * size)
    group = heads // kv_local
    total = own[...]
    for part in parts:
        total = total + part[...].astype(F32)
    fresh = total.astype(BF16)
    fresh_out[...] = fresh
    keys = jnp.concatenate([fresh[:, 2 * k * size:(2 * k + 1) * size] for k in range(kv_local)], axis=0)
    values = jnp.concatenate([fresh[:, (2 * k + 1) * size:(2 * k + 2) * size] for k in range(kv_local)], axis=0)
    scores = dot_t(queries[...].reshape(count * heads, size), keys) * size ** -0.5
    col = lax.broadcasted_iota(jnp.int32, scores.shape, 1)
    row = lax.broadcasted_iota(jnp.int32, scores.shape, 0)
    token, other = row // heads, col % count
    valid = (
        (token // steps_new == other // steps_new)
        & (other <= token)
        & (row % heads // group == col // count)
    )
    scores = jnp.where(valid, scores, -1e30)
    stat = stat_in[...]
    top_before, total_before = stat[:, :1], stat[:, 1:2]
    top = jnp.maximum(top_before, jnp.max(scores, axis=1, keepdims=True))
    weights = jnp.exp(scores - top)
    keep = jnp.exp(top_before - top)
    norm = 1.0 / (total_before * keep + jnp.sum(weights, axis=1, keepdims=True))
    mixed = acc_in[...] * keep + dot(weights.astype(BF16), values)
    scratch[...] = mixed * norm
    for h in range(heads):
        attended[:, h * size:(h + 1) * size] = scratch[pl.ds(h, count, stride=heads), :].astype(BF16)


def body(
    hidden,
    queries,
    cache,
    key_value_weight,
    adapter_down_weight,
    adapter_up_key,
    adapter_up_value,
    request_adapter,
    adapter_storage,
    lengths,
):
    pool, tensor = lax.axis_size("pool"), lax.axis_size("tensor")
    p, t = lax.axis_index("pool"), lax.axis_index("tensor")
    rows, steps_new, width = hidden.shape
    count = rows * steps_new
    part = width // pool
    down_here, up_here = adapter_down_weight.shape[0], adapter_up_key.shape[0]
    _, kv_local, pair = key_value_weight.shape
    heads, size = queries.shape[2:]
    assert adapter_storage.shape[0] <= 256 and pool & (pool - 1) == 0 and tensor & (tensor - 1) == 0
    assert pool % tensor == 0 and down_here == up_here * (pool // tensor)
    parts = 2 if tensor % 2 == 0 else 1
    half = part // parts
    side = t % parts
    place = jnp.stack([p, side, t * down_here, p * up_here]).astype(jnp.int32)

    def over_pool(x, k):
        return lax.ppermute(x, "pool", [(i, i ^ k) for i in range(pool)])

    def over_pair(x):
        return lax.ppermute(x, "tensor", [(i, i ^ 1) for i in range(tensor)])

    chunk = struct((count, half + LANES), BF16)
    packed = pl.pallas_call(
        functools.partial(pack_kernel, pool, parts),
        out_shape=[chunk] * pool + [struct((count, half), BF16)] * (parts - 1),
        in_specs=[SMEM, SMEM, SMEM, VMEM],
        out_specs=[VMEM] * (pool + parts - 1),
        name="pack",
        cost_estimate=cost(0, 2 * hidden.size * 2),
    )(place, request_adapter, adapter_storage, hidden)
    chunks = [packed[0]] + [None] * (pool - 1)
    for k in range(pool - 1, 0, -1):
        chunks[k] = over_pool(packed[k], k)
    operands = list(chunks)
    if parts == 2:
        swapped = [None] * pool
        for k in range(pool - 1, 0, -1):
            swapped[k] = over_pair(chunks[k])
        operands += [packed[pool]] + swapped[1:]

    acc, stat = attend_cache(lengths, queries, cache)

    weight = jnp.transpose(key_value_weight, (1, 0, 2))
    all_rows = pool * count
    base, slots, shrink = pl.pallas_call(
        functools.partial(project_kernel, pool, parts),
        out_shape=[
            struct((all_rows, kv_local * pair), F32),
            struct((all_rows, LANES), BF16),
            struct((all_rows, LANES), BF16),
        ],
        in_specs=[SMEM] + [VMEM] * (len(operands) + 2),
        out_specs=[VMEM] * 3,
        name="project",
        cost_estimate=cost(2 * all_rows * part * (kv_local * pair + down_here * LANES), 6 << 20),
    )(place, *operands, weight, adapter_down_weight)

    ratio = pool // tensor
    mine = None
    for j in range(ratio):
        for m in range(0, tensor, parts):
            pairs = [
                (i * tensor + s, (s * ratio + ((i // tensor) ^ j)) * tensor + ((i % tensor) ^ m))
                for i in range(pool)
                for s in range(tensor)
            ]
            moved = lax.ppermute(shrink, ("pool", "tensor"), pairs).astype(F32)
            mine = moved if mine is None else mine + moved
    sums = [mine] + ([over_pair(mine)] if parts == 2 else [])
    expanded = pl.pallas_call(
        functools.partial(expand_kernel, pool, parts),
        out_shape=[struct((count, kv_local * pair), F32)] + [struct((count, kv_local * pair), BF16)] * (pool - 1),
        in_specs=[SMEM] + [VMEM] * (parts + 4),
        out_specs=[VMEM] * pool,
        scratch_shapes=[pltpu.VMEM((all_rows, LANES), F32)],
        name="expand",
        cost_estimate=cost(4 * all_rows * LANES * up_here * LANES, 1 << 20),
    )(place, *sums, slots, base, adapter_up_key, adapter_up_value)
    received = [None] * pool
    for k in range(pool - 1, 0, -1):
        received[k] = over_pool(expanded[k], k)
    attended, fresh = pl.pallas_call(
        functools.partial(finish_kernel, pool),
        out_shape=[struct((count, heads * size), BF16), struct((count, kv_local * pair), BF16)],
        in_specs=[VMEM] * (pool + 3),
        out_specs=[VMEM] * 2,
        scratch_shapes=[pltpu.VMEM((count * heads, size), F32)],
        name="finish",
        cost_estimate=cost(4 * count * heads * size * LANES, 1 << 20),
    )(expanded[0], *received[1:], queries, acc, stat)
    return (
        attended.reshape(rows, steps_new, heads * size),
        fresh.reshape(rows, steps_new, kv_local, pair),
    )


def attend_cache(lengths, queries, cache):
    rows, steps_new, heads, size = queries.shape
    depth, kv_local = cache.shape[1], cache.shape[2]
    rows_step = 4 if rows % 4 == 0 else 1
    block = rows_step * steps_new * heads
    return pl.pallas_call(
        functools.partial(cache_kernel, rows_step),
        out_shape=[struct((rows * steps_new * heads, size), F32), struct((rows * steps_new * heads, LANES), F32)],
        grid=(rows // rows_step,),
        in_specs=[
            SMEM,
            pl.BlockSpec((rows_step, steps_new, heads, size), lambda i: (i, 0, 0, 0)),
            pl.BlockSpec((rows_step, depth, kv_local, 2 * size), lambda i: (i, 0, 0, 0)),
        ],
        out_specs=[pl.BlockSpec((block, size), lambda i: (i, 0)), pl.BlockSpec((block, LANES), lambda i: (i, 0))],
        name="cached",
        cost_estimate=cost(8 * rows * steps_new * heads * depth * kv_local * size, cache.size * 2),
    )(lengths, queries, cache)


def solution(mesh):
    return jax.shard_map(
        body,
        mesh=mesh,
        in_specs=(
            P(("groups", "pool"), None, None),
            P(("groups", "pool"), None, "tensor", None),
            P(("groups", "pool"), None, "tensor", None),
            P("pool", "tensor", None),
            P("tensor", "pool", None),
            P("pool", None, "tensor", None),
            P("pool", None, "tensor", None),
            P(("groups", "pool")),
            P(),
            P(("groups", "pool")),
        ),
        out_specs=(
            P(("groups", "pool"), None, "tensor"),
            P(("groups", "pool"), None, "tensor", None),
        ),
        check_vma=False,
    )
```

```python
import functools
import jax
import jax.numpy as jnp
from jax import lax
from jax.experimental import pallas as pl
from jax.experimental.pallas import tpu as pltpu
from jax.sharding import PartitionSpec as P

ADAPTER_SCALE = 0.5
LANES = 128
F32 = jnp.float32
BF16 = jnp.bfloat16
VMEM = pl.BlockSpec(memory_space=pltpu.VMEM)
SMEM = pl.BlockSpec(memory_space=pltpu.SMEM)
HBM = pl.BlockSpec(memory_space=pltpu.HBM)
ANY = pl.BlockSpec(memory_space=pl.ANY)
LIMIT = 16 * 1024 * 1024
TOKEN = jax.ShapeDtypeStruct((8, LANES), F32)
PACK = 62 * 1024 * 1024


def dot(a, b):
    return jnp.dot(a, b, preferred_element_type=F32)


def dot_t(a, b):
    return lax.dot_general(a, b, (((1,), (1,)), ((), ())), preferred_element_type=F32)


def struct(shape, dtype):
    return jax.ShapeDtypeStruct(shape, dtype)


def cost(flops, moved):
    return pl.CostEstimate(flops=int(flops), bytes_accessed=int(moved), transcendentals=0)


def pack_kernel(pool, parts, request_adapter, adapter_storage, lengths, hidden, *refs):
    outs, (spans, pieces, ids, table, sizes, sems) = refs[:pool + parts - 1], refs[pool + parts - 1:]
    rows, steps_new, width = hidden.shape
    count = rows * steps_new
    part = width // pool
    half = part // parts
    me, side = lax.axis_index("pool"), lax.axis_index("tensor") % parts
    copies = [
        pltpu.make_async_copy(request_adapter, ids, sems.at[0]),
        pltpu.make_async_copy(adapter_storage, table, sems.at[1]),
        pltpu.make_async_copy(lengths, sizes, sems.at[2]),
    ]
    starts = [(me ^ k) * part + side * half for k in range(pool)] + [me * part + (1 - side) * half]
    for k in range(pool + parts - 1):
        at = pl.ds(pl.multiple_of(starts[k], LANES), half)
        copies.append(pltpu.make_async_copy(hidden.at[:, :, at], pieces.at[k], sems.at[3 + k]))
    for c in copies:
        c.start()
    copies[0].wait()
    copies[1].wait()
    copies[2].wait()
    row = lax.broadcasted_iota(jnp.int32, (count, LANES), 0) // steps_new
    slots = jnp.zeros((count, LANES), jnp.int32)
    for r in range(rows):
        slots = jnp.where(row == r, table[ids[r]], slots)
    slots = slots.astype(F32).astype(BF16)
    request = lax.broadcasted_iota(jnp.int32, spans.shape, 0)
    reach = jnp.zeros(spans.shape, jnp.int32)
    for r in range(rows):
        reach = jnp.where(request == r, sizes[r], reach)
    spans[...] = reach
    for k in range(pool + parts - 1):
        copies[3 + k].wait()
        outs[k][:, :half] = pieces[k].reshape(count, half)
        if k < pool:
            outs[k][:, half:] = slots


def both_sides(pool, parts, refs):
    chunks = refs[:pool]
    half = chunks[0].shape[1] - LANES
    side = lax.axis_index("tensor") % parts
    sides = [(side * half, jnp.concatenate([c[:, :half] for c in chunks], axis=0))]
    if parts == 2:
        rest = [refs[pool][...]] + [c[:, :half] for c in refs[pool + 1:2 * pool]]
        sides.append(((1 - side) * half, jnp.concatenate(rest, axis=0)))
    return [(pl.ds(pl.multiple_of(start, half), half), x) for start, x in sides]


def shrink_kernel(pool, parts, *refs):
    down, shrink, slots_out, token = refs[parts * pool:]
    token[...] = jnp.zeros_like(token)
    count = refs[0].shape[0]
    half = refs[0].shape[1] - LANES
    me = lax.axis_index("pool")
    first_slot = lax.axis_index("tensor") * down.shape[0]
    sides = both_sides(pool, parts, refs)
    slots = jnp.concatenate([c[:, half:] for c in refs[:pool]], axis=0)
    slots_out[...] = slots
    slots = slots.astype(F32)
    step = 2 if down.shape[0] % 2 == 0 else 1
    total = jnp.zeros((count * pool, LANES), F32)
    for a in range(0, down.shape[0], step):
        out = 0.0
        for at, x in sides:
            out += dot(x, jnp.concatenate([down[a + i, at, :] for i in range(step)], axis=1))
        for i in range(step):
            match = slots == (first_slot + a + i).astype(F32)
            total = jnp.where(match, out[:, i * LANES:(i + 1) * LANES], total)
    total = total.astype(BF16)
    for k in range(pool):
        at = pl.ds(pl.multiple_of((me ^ k) * count, count), count)
        shrink[at, :] = total[k * count:(k + 1) * count]


def base_kernel(pool, parts, *refs):
    weight, _, base = refs[parts * pool:]
    sides = both_sides(pool, parts, refs)
    for k in range(weight.shape[0]):
        out = 0.0
        for at, x in sides:
            out += dot(x, weight[k, at, :])
        base[:, k * weight.shape[2]:(k + 1) * weight.shape[2]] = out


def expand_kernel(pool, parts, *refs):
    sums, refs = refs[:parts], refs[parts:]
    slots_in, base, up_key, up_value = refs[:4]
    outs, token, scratch = refs[4:4 + pool], refs[4 + pool], refs[5 + pool]
    token[...] = jnp.zeros_like(token)
    holders, rank, kv_local, size = up_key.shape
    me = lax.axis_index("pool")
    first_slot = me * holders
    count = base.shape[0] // pool
    total = sums[0][...]
    for s in sums[1:]:
        total = total + s[...]
    scratch[...] = total
    ordered = jnp.concatenate(
        [scratch[pl.ds(pl.multiple_of((me ^ k) * count, count), count), :] for k in range(pool)], axis=0
    ).astype(BF16)
    slots = slots_in[...].astype(F32)
    deep = rank * kv_local
    for which, up in ((0, up_key), (1, up_value)):
        row = lax.broadcasted_iota(jnp.int32, (2 * rank, deep), 0)
        col = lax.broadcasted_iota(jnp.int32, (2 * rank, deep), 1)
        wide = []
        for k in range(kv_local):
            pick = (row == which * rank + col // kv_local) & (col % kv_local == k)
            wide.append(dot(ordered, pick.astype(F32).astype(BF16)))
        acc = [jnp.zeros((base.shape[0], size), F32) for _ in range(kv_local)]
        for a in range(holders):
            match = slots == (first_slot + a).astype(F32)
            if deep != LANES:
                match = match[:, :1]
            table = up[a].reshape(deep, size)
            for k in range(kv_local):
                acc[k] = acc[k] + dot(jnp.where(match, wide[k], 0.0).astype(BF16), table)
        for k in range(kv_local):
            at = slice((2 * k + which) * size, (2 * k + which + 1) * size)
            value = base[:, at] + ADAPTER_SCALE * acc[k]
            outs[0][:, at] = value[:count]
            for j in range(1, pool):
                outs[j][:, at] = value[j * count:(j + 1) * count].astype(BF16)


def cache_kernel(spans, queries, cache, _, acc_out, stat_out, scores_all, weights_all):
    rows, steps_new, heads, size = queries.shape
    kv_local, depth = cache.shape[1:3]
    count = steps_new * heads
    which = lax.broadcasted_iota(jnp.int32, (count, 1), 0) % heads // (heads // kv_local)
    col = lax.broadcasted_iota(jnp.int32, (1, depth), 1)
    for r in range(rows):
        q = queries[r].reshape(count, size)
        scores = dot_t(q, cache[r, 0, :, :size])
        for k in range(1, kv_local):
            scores = jnp.where(which == k, dot_t(q, cache[r, k, :, :size]), scores)
        scores = jnp.where(col < spans[r:r + 1, :], scores * size ** -0.5, -1e30)
        scores_all[r * count:(r + 1) * count, :] = scores
    scores = scores_all[...]
    top = jnp.max(scores, axis=1, keepdims=True)
    weights = jnp.exp(scores - top)
    total = jnp.sum(weights, axis=1, keepdims=True)
    lane = lax.broadcasted_iota(jnp.int32, (rows * count, LANES), 1)
    stat_out[...] = jnp.where(lane == 0, top, total)
    weights_all[...] = weights.astype(BF16)
    for r in range(rows):
        weights = weights_all[r * count:(r + 1) * count, :]
        mixed = dot(weights, cache[r, 0, :, size:])
        for k in range(1, kv_local):
            mixed = jnp.where(which == k, dot(weights, cache[r, k, :, size:]), mixed)
        acc_out[r * count:(r + 1) * count, :] = mixed


def finish_kernel(pool, own, *refs):
    parts, refs = refs[:pool - 1], refs[pool - 1:]
    queries, acc, stat, attended, fresh_out, scratch = refs
    rows, steps_new, heads, size = queries.shape
    count = rows * steps_new
    kv_local = own.shape[1] // (2 * size)
    group = heads // kv_local
    total = own[...]
    for part in parts:
        total = total + part[...].astype(F32)
    fresh = total.astype(BF16)
    wide = 2 * size
    fresh_out[...] = jnp.stack([fresh[:, k * wide:(k + 1) * wide] for k in range(kv_local)], axis=1).reshape(fresh_out.shape)
    keys = jnp.concatenate([fresh[:, 2 * k * size:(2 * k + 1) * size] for k in range(kv_local)], axis=0)
    values = jnp.concatenate([fresh[:, (2 * k + 1) * size:(2 * k + 2) * size] for k in range(kv_local)], axis=0)
    scores = dot_t(queries[...].reshape(count * heads, size), keys) * size ** -0.5
    col = lax.broadcasted_iota(jnp.int32, scores.shape, 1)
    row = lax.broadcasted_iota(jnp.int32, scores.shape, 0)
    token, other = row // heads, col % count
    valid = (
        (token // steps_new == other // steps_new)
        & (other <= token)
        & (row % heads // group == col // count)
    )
    scores = jnp.where(valid, scores, -1e30)
    stat = stat[...]
    top_before, total_before = stat[:, :1], stat[:, 1:2]
    top = jnp.maximum(top_before, jnp.max(scores, axis=1, keepdims=True))
    weights = jnp.exp(scores - top)
    keep = jnp.exp(top_before - top)
    norm = 1.0 / (total_before * keep + jnp.sum(weights, axis=1, keepdims=True))
    mixed = acc[...] * keep + dot(weights.astype(BF16), values)
    scratch[...] = mixed * norm
    for h in range(heads):
        out = scratch[pl.ds(h, count, stride=heads), :].astype(BF16)
        attended[:, :, h * size:(h + 1) * size] = out.reshape(rows, steps_new, size)


def body(
    hidden,
    queries,
    cache,
    key_value_weight,
    adapter_down_weight,
    adapter_up_key,
    adapter_up_value,
    request_adapter,
    adapter_storage,
    lengths,
):
    pool, tensor = lax.axis_size("pool"), lax.axis_size("tensor")
    rows, steps_new, width = hidden.shape
    count = rows * steps_new
    part = width // pool
    down_here, up_here = adapter_down_weight.shape[0], adapter_up_key.shape[0]
    _, kv_local, pair = key_value_weight.shape
    heads, size = queries.shape[2:]
    assert adapter_storage.shape[0] <= 256 and pool & (pool - 1) == 0 and tensor & (tensor - 1) == 0
    assert pool % tensor == 0 and down_here == up_here * (pool // tensor)
    parts = 2 if tensor % 2 == 0 else 1
    half = part // parts

    def over_pool(x, k):
        return lax.ppermute(x, "pool", [(i, i ^ k) for i in range(pool)])

    def over_pair(x):
        return lax.ppermute(x, "tensor", [(i, i ^ 1) for i in range(tensor)])

    def call(name, kernel, operands, in_specs, outs, scratch=(), work=0, moved=1 << 20, limit=LIMIT):
        return pl.pallas_call(
            kernel,
            out_shape=outs,
            in_specs=in_specs,
            out_specs=[VMEM] * len(outs),
            scratch_shapes=scratch,
            name=name,
            compiler_params=pltpu.CompilerParams(vmem_limit_bytes=limit),
            cost_estimate=cost(work, moved),
        )(*operands)

    chunk = struct((count, half + LANES), BF16)
    packed = call(
        "pack",
        functools.partial(pack_kernel, pool, parts),
        (request_adapter, adapter_storage, lengths, hidden),
        [HBM] * 4,
        [chunk] * pool + [struct((count, half), BF16)] * (parts - 1) + [struct((rows, cache.shape[1]), jnp.int32)],
        [
            pltpu.VMEM((pool + parts - 1, rows, steps_new, half), BF16),
            pltpu.SMEM(request_adapter.shape, jnp.int32),
            pltpu.SMEM(adapter_storage.shape, jnp.int32),
            pltpu.SMEM(lengths.shape, jnp.int32),
            pltpu.SemaphoreType.DMA((pool + parts + 2,)),
        ],
        limit=PACK,
    )
    operands = [packed[0]] + [None] * (pool - 1)
    for k in range(pool - 1, 0, -1):
        operands[k] = over_pool(packed[k], k)
    stored, _ = lax.optimization_barrier((cache, packed[0]))
    stored = jnp.transpose(stored, (0, 2, 1, 3))
    if parts == 2:
        swapped = [None] * pool
        for k in range(pool - 1, 0, -1):
            operands[k], stored = lax.optimization_barrier((operands[k], stored))
            swapped[k] = over_pair(operands[k])
        operands += [packed[pool]] + swapped[1:]

    all_rows = pool * count
    chunks_in = [VMEM] * len(operands)
    shrink, slots, token = call(
        "shrink",
        functools.partial(shrink_kernel, pool, parts),
        (*operands, adapter_down_weight),
        chunks_in + [VMEM],
        [struct((all_rows, LANES), BF16)] * 2 + [TOKEN],
        work=2 * all_rows * part * down_here * LANES,
        moved=4 << 20,
    )
    weight, marked = lax.optimization_barrier((key_value_weight, token))
    (base,) = call(
        "base",
        functools.partial(base_kernel, pool, parts),
        (*operands, jnp.transpose(weight, (1, 0, 2)), marked),
        chunks_in + [VMEM, ANY],
        [struct((all_rows, kv_local * pair), F32)],
        work=2 * all_rows * part * kv_local * pair,
        moved=3 << 20,
    )

    ratio = pool // tensor
    mine = None
    for j in range(ratio):
        for m in range(0, tensor, parts):
            pairs = [
                (i * tensor + s, (s * ratio + ((i // tensor) ^ j)) * tensor + ((i % tensor) ^ m))
                for i in range(pool)
                for s in range(tensor)
            ]
            moved = lax.ppermute(shrink, ("pool", "tensor"), pairs).astype(F32)
            mine = moved if mine is None else mine + moved
    sums = [mine] + ([over_pair(mine)] if parts == 2 else [])
    expanded = call(
        "expand",
        functools.partial(expand_kernel, pool, parts),
        (*sums, slots, base, adapter_up_key, adapter_up_value),
        [VMEM] * (parts + 4),
        [struct((count, kv_local * pair), F32)] + [struct((count, kv_local * pair), BF16)] * (pool - 1) + [TOKEN],
        [pltpu.VMEM((all_rows, LANES), F32)],
        work=4 * all_rows * LANES * up_here * LANES,
    )
    received = [None] * pool
    for k in range(pool - 1, 0, -1):
        received[k] = over_pool(expanded[k], k)
    acc, stat = call(
        "cached",
        cache_kernel,
        (packed[-1], queries, stored, expanded[pool]),
        [VMEM] * 3 + [ANY],
        [struct((count * heads, n), F32) for n in (size, LANES)],
        [pltpu.VMEM((count * heads, cache.shape[1]), t) for t in (F32, BF16)],
        work=4 * count * heads * cache.shape[1] * kv_local * size,
        moved=cache.size * 2,
    )
    return tuple(call(
        "finish",
        functools.partial(finish_kernel, pool),
        (expanded[0], *received[1:], queries, acc, stat),
        [VMEM] * (pool + 3),
        [struct((rows, steps_new, heads * size), BF16), struct((rows, steps_new, kv_local, pair), BF16)],
        [pltpu.VMEM((count * heads, size), F32)],
        work=4 * count * heads * size * LANES,
    ))


def solution(mesh):
    return jax.shard_map(
        body,
        mesh=mesh,
        in_specs=(
            P(("groups", "pool"), None, None),
            P(("groups", "pool"), None, "tensor", None),
            P(("groups", "pool"), None, "tensor", None),
            P("pool", "tensor", None),
            P("tensor", "pool", None),
            P("pool", None, "tensor", None),
            P("pool", None, "tensor", None),
            P(("groups", "pool")),
            P(),
            P(("groups", "pool")),
        ),
        out_specs=(
            P(("groups", "pool"), None, "tensor"),
            P(("groups", "pool"), None, "tensor", None),
        ),
        check_vma=False,
    )
```

```python
import functools
import jax
import jax.numpy as jnp
from jax import lax
from jax.experimental import pallas as pl
from jax.experimental.pallas import tpu as pltpu
from jax.sharding import PartitionSpec as P

ADAPTER_SCALE = 0.5
LANES = 128
F32 = jnp.float32
BF16 = jnp.bfloat16
VMEM = pl.BlockSpec(memory_space=pltpu.VMEM)
SMEM = pl.BlockSpec(memory_space=pltpu.SMEM)
HBM = pl.BlockSpec(memory_space=pltpu.HBM)
ANY = pl.BlockSpec(memory_space=pl.ANY)
LIMIT = 16 * 1024 * 1024
WHOLE = (0, 1)
TAIL = 16
TOKEN = jax.ShapeDtypeStruct((8, LANES), F32)
PACK = 62 * 1024 * 1024


def dot(a, b):
    return jnp.dot(a, b, preferred_element_type=F32)


def dot_t(a, b):
    return lax.dot_general(a, b, (((1,), (1,)), ((), ())), preferred_element_type=F32)


def struct(shape, dtype):
    return jax.ShapeDtypeStruct(shape, dtype)


def cost(flops, moved):
    return pl.CostEstimate(flops=int(flops), bytes_accessed=int(moved), transcendentals=0)


def pack_kernel(pool, parts, request_adapter, adapter_storage, lengths, hidden, *refs):
    outs, (spans, pieces, ids, table, sizes, sems) = refs[:pool], refs[pool:]
    rows, steps_new, width = hidden.shape
    count = rows * steps_new
    part = width // pool
    half = part // parts
    me, side = lax.axis_index("pool"), lax.axis_index("tensor") % parts
    copies = [
        pltpu.make_async_copy(request_adapter, ids, sems.at[0]),
        pltpu.make_async_copy(adapter_storage, table, sems.at[1]),
        pltpu.make_async_copy(lengths, sizes, sems.at[2]),
    ]
    places = []
    for k in reversed(range(pool)):
        for i in range(parts if k in WHOLE else 1):
            start = (me ^ k) * part + (side if i == 0 else 1 - side) * half
            source = hidden.at[:, :, pl.ds(pl.multiple_of(start, LANES), half)]
            copies.append(pltpu.make_async_copy(source, pieces.at[len(places)], sems.at[3 + len(places)]))
            places.append((k, i * half // LANES))
    for c in copies:
        c.start()
    for c in copies[:3]:
        c.wait()
    lane = lax.broadcasted_iota(jnp.int32, (TAIL, LANES), 1) // steps_new
    slots = jnp.zeros((TAIL, LANES), jnp.int32)
    for r in range(rows):
        slots = jnp.where(lane == r, table[ids[r]], slots)
    slots = slots.astype(F32).astype(BF16)
    request = lax.broadcasted_iota(jnp.int32, spans.shape, 0)
    reach = jnp.zeros(spans.shape, jnp.int32)
    for r in range(rows):
        reach = jnp.where(request == r, sizes[r], reach)
    spans[...] = reach
    for k in range(pool):
        outs[k][-TAIL:, :] = slots
    for n, (k, first) in enumerate(places):
        copies[3 + n].wait()
        piece = pieces[n].reshape(count, half)
        for j in range(half // LANES):
            outs[k][(first + j) * count:(first + j + 1) * count, :] = piece[:, j * LANES:(j + 1) * LANES]


def both_sides(pool, parts, count, half, refs):
    side = lax.axis_index("tensor") % parts
    tiles = half // LANES

    def rows(chunk, first):
        return jnp.concatenate([chunk[j * count:(j + 1) * count, :] for j in range(first, first + tiles)], axis=1)

    sides = [(side * half, jnp.concatenate([rows(c, 0) for c in refs[:pool]], axis=0))]
    if parts == 2:
        swapped = iter(refs[pool:])
        rest = [rows(refs[k], tiles) if k in WHOLE else rows(next(swapped), 0) for k in range(pool)]
        sides.append(((1 - side) * half, jnp.concatenate(rest, axis=0)))
    return [(pl.ds(pl.multiple_of(start, half), half), x) for start, x in sides]


def shrink_kernel(pool, parts, count, half, *refs):
    down, shrink, slots_out, token = refs[-4:]
    token[...] = jnp.zeros_like(token)
    me = lax.axis_index("pool")
    first_slot = lax.axis_index("tensor") * down.shape[0]
    sides = both_sides(pool, parts, count, half, refs[:-4])
    row = lax.broadcasted_iota(jnp.int32, (count, LANES), 0)
    lane = lax.broadcasted_iota(jnp.int32, (count, LANES), 1)
    slots = []
    for c in refs[:pool]:
        line = c[-TAIL:, :].astype(F32)[:1, :]
        slots.append(jnp.sum(jnp.where(row == lane, line, 0.0), axis=1, keepdims=True))
    slots = jnp.broadcast_to(jnp.concatenate(slots, axis=0), (count * pool, LANES))
    slots_out[...] = slots
    step = 2 if down.shape[0] % 2 == 0 else 1
    total = jnp.zeros((count * pool, LANES), F32)
    for a in range(0, down.shape[0], step):
        out = 0.0
        for at, x in sides:
            out += dot(x, jnp.concatenate([down[a + i, at, :] for i in range(step)], axis=1))
        for i in range(step):
            match = slots == (first_slot + a + i).astype(F32)
            total = jnp.where(match, out[:, i * LANES:(i + 1) * LANES], total)
    total = total.astype(BF16)
    for k in range(pool):
        at = pl.ds(pl.multiple_of((me ^ k) * count, count), count)
        shrink[at, :] = total[k * count:(k + 1) * count]


def base_kernel(pool, parts, count, half, *refs):
    weight, _, base = refs[-3:]
    sides = both_sides(pool, parts, count, half, refs[:-3])
    for k in range(weight.shape[0]):
        out = 0.0
        for at, x in sides:
            out += dot(x, weight[k, at, :])
        base[:, k * weight.shape[2]:(k + 1) * weight.shape[2]] = out


def expand_kernel(pool, parts, *refs):
    sums, refs = refs[:parts], refs[parts:]
    slots_in, base, up_key, up_value = refs[:4]
    outs, token, scratch = refs[4:4 + pool], refs[4 + pool], refs[5 + pool]
    token[...] = jnp.zeros_like(token)
    holders, rank, kv_local, size = up_key.shape
    me = lax.axis_index("pool")
    first_slot = me * holders
    count = base.shape[0] // pool
    total = sums[0][...]
    for s in sums[1:]:
        total = total + s[...]
    scratch[...] = total
    ordered = jnp.concatenate(
        [scratch[pl.ds(pl.multiple_of((me ^ k) * count, count), count), :] for k in range(pool)], axis=0
    ).astype(BF16)
    slots = slots_in[...]
    deep = rank * kv_local
    for which, up in ((0, up_key), (1, up_value)):
        row = lax.broadcasted_iota(jnp.int32, (2 * rank, deep), 0)
        col = lax.broadcasted_iota(jnp.int32, (2 * rank, deep), 1)
        wide = []
        for k in range(kv_local):
            pick = (row == which * rank + col // kv_local) & (col % kv_local == k)
            wide.append(dot(ordered, pick.astype(F32).astype(BF16)))
        acc = [jnp.zeros((base.shape[0], size), F32) for _ in range(kv_local)]
        for a in range(holders):
            match = slots == (first_slot + a).astype(F32)
            if deep != LANES:
                match = match[:, :1]
            table = up[a].reshape(deep, size)
            for k in range(kv_local):
                acc[k] = acc[k] + dot(jnp.where(match, wide[k], 0.0).astype(BF16), table)
        for k in range(kv_local):
            at = slice((2 * k + which) * size, (2 * k + which + 1) * size)
            value = base[:, at] + ADAPTER_SCALE * acc[k]
            outs[0][:, at] = value[:count]
            for j in range(1, pool):
                outs[j][:, at] = value[j * count:(j + 1) * count].astype(BF16)


def cache_kernel(spans, queries, cache, _, acc_out, stat_out, scores_all, weights_all):
    rows, steps_new, heads, size = queries.shape
    kv_local, depth = cache.shape[1:3]
    count = steps_new * heads
    which = lax.broadcasted_iota(jnp.int32, (count, 1), 0) % heads // (heads // kv_local)
    col = lax.broadcasted_iota(jnp.int32, (1, depth), 1)
    for r in range(rows):
        q = queries[r].reshape(count, size)
        scores = dot_t(q, cache[r, 0, :, :size])
        for k in range(1, kv_local):
            scores = jnp.where(which == k, dot_t(q, cache[r, k, :, :size]), scores)
        scores = jnp.where(col < spans[r:r + 1, :], scores * size ** -0.5, -1e30)
        scores_all[r * count:(r + 1) * count, :] = scores
    scores = scores_all[...]
    top = jnp.max(scores, axis=1, keepdims=True)
    weights = jnp.exp(scores - top)
    total = jnp.sum(weights, axis=1, keepdims=True)
    lane = lax.broadcasted_iota(jnp.int32, (rows * count, LANES), 1)
    stat_out[...] = jnp.where(lane == 0, top, total)
    weights_all[...] = weights.astype(BF16)
    for r in range(rows):
        weights = weights_all[r * count:(r + 1) * count, :]
        mixed = dot(weights, cache[r, 0, :, size:])
        for k in range(1, kv_local):
            mixed = jnp.where(which == k, dot(weights, cache[r, k, :, size:]), mixed)
        acc_out[r * count:(r + 1) * count, :] = mixed


def finish_kernel(pool, own, *refs):
    parts, refs = refs[:pool - 1], refs[pool - 1:]
    queries, acc, stat, attended, fresh_out, scratch = refs
    rows, steps_new, heads, size = queries.shape
    count = rows * steps_new
    kv_local = own.shape[1] // (2 * size)
    group = heads // kv_local
    total = own[...]
    for part in parts:
        total = total + part[...].astype(F32)
    fresh = total.astype(BF16)
    wide = 2 * size
    fresh_out[...] = jnp.stack([fresh[:, k * wide:(k + 1) * wide] for k in range(kv_local)], axis=1).reshape(fresh_out.shape)
    keys = jnp.concatenate([fresh[:, 2 * k * size:(2 * k + 1) * size] for k in range(kv_local)], axis=0)
    values = jnp.concatenate([fresh[:, (2 * k + 1) * size:(2 * k + 2) * size] for k in range(kv_local)], axis=0)
    scores = dot_t(queries[...].reshape(count * heads, size), keys) * size ** -0.5
    col = lax.broadcasted_iota(jnp.int32, scores.shape, 1)
    row = lax.broadcasted_iota(jnp.int32, scores.shape, 0)
    token, other = row // heads, col % count
    valid = (
        (token // steps_new == other // steps_new)
        & (other <= token)
        & (row % heads // group == col // count)
    )
    scores = jnp.where(valid, scores, -1e30)
    stat = stat[...]
    top_before, total_before = stat[:, :1], stat[:, 1:2]
    top = jnp.maximum(top_before, jnp.max(scores, axis=1, keepdims=True))
    weights = jnp.exp(scores - top)
    keep = jnp.exp(top_before - top)
    norm = 1.0 / (total_before * keep + jnp.sum(weights, axis=1, keepdims=True))
    mixed = acc[...] * keep + dot(weights.astype(BF16), values)
    scratch[...] = mixed * norm
    for h in range(heads):
        out = scratch[pl.ds(h, count, stride=heads), :].astype(BF16)
        attended[:, :, h * size:(h + 1) * size] = out.reshape(rows, steps_new, size)


def body(
    hidden,
    queries,
    cache,
    key_value_weight,
    adapter_down_weight,
    adapter_up_key,
    adapter_up_value,
    request_adapter,
    adapter_storage,
    lengths,
):
    pool, tensor = lax.axis_size("pool"), lax.axis_size("tensor")
    rows, steps_new, width = hidden.shape
    count = rows * steps_new
    part = width // pool
    down_here, up_here = adapter_down_weight.shape[0], adapter_up_key.shape[0]
    _, kv_local, pair = key_value_weight.shape
    heads, size = queries.shape[2:]
    assert adapter_storage.shape[0] <= 256 and count <= LANES and pool & (pool - 1) == 0 and tensor & (tensor - 1) == 0
    assert pool % tensor == 0 and down_here == up_here * (pool // tensor)
    parts = 2 if tensor % 2 == 0 else 1
    half = part // parts

    def over_pool(x, k):
        return lax.ppermute(x, "pool", [(i, i ^ k) for i in range(pool)])

    def over_pair(x):
        return lax.ppermute(x, "tensor", [(i, i ^ 1) for i in range(tensor)])

    def call(name, kernel, operands, in_specs, outs, scratch=(), work=0, moved=1 << 20, limit=LIMIT):
        return pl.pallas_call(
            kernel,
            out_shape=outs,
            in_specs=in_specs,
            out_specs=[VMEM] * len(outs),
            scratch_shapes=scratch,
            name=name,
            compiler_params=pltpu.CompilerParams(vmem_limit_bytes=limit),
            cost_estimate=cost(work, moved),
        )(*operands)

    chunks = [
        struct((count * (part if k in WHOLE else half) // LANES + TAIL, LANES), BF16) for k in range(pool)
    ]
    pieces = sum(parts if k in WHOLE else 1 for k in range(pool))
    packed = call(
        "pack",
        functools.partial(pack_kernel, pool, parts),
        (request_adapter, adapter_storage, lengths, hidden),
        [HBM] * 4,
        chunks + [struct((rows, cache.shape[1]), jnp.int32)],
        [
            pltpu.VMEM((pieces, rows, steps_new, half), BF16),
            pltpu.SMEM(request_adapter.shape, jnp.int32),
            pltpu.SMEM(adapter_storage.shape, jnp.int32),
            pltpu.SMEM(lengths.shape, jnp.int32),
            pltpu.SemaphoreType.DMA((3 + pieces,)),
        ],
        limit=PACK,
    )
    operands = [packed[0]] + [None] * (pool - 1)
    for k in range(pool - 1, 0, -1):
        operands[k] = over_pool(packed[k], k)
    stored, _ = lax.optimization_barrier((cache, packed[0]))
    stored = jnp.transpose(stored, (0, 2, 1, 3))
    swapped = {}
    for k in [*range(2, pool), 1]:
        operands[k], stored = lax.optimization_barrier((operands[k], stored))
        if parts == 2 and k not in WHOLE:
            swapped[k] = over_pair(operands[k])
    operands += [swapped[k] for k in sorted(swapped)]

    all_rows = pool * count
    chunks_in = [VMEM] * len(operands)
    shrink, slots, token = call(
        "shrink",
        functools.partial(shrink_kernel, pool, parts, count, half),
        (*operands, adapter_down_weight),
        chunks_in + [VMEM],
        [struct((all_rows, LANES), BF16), struct((all_rows, LANES), F32), TOKEN],
        work=2 * all_rows * part * down_here * LANES,
        moved=4 << 20,
    )
    weight, marked = lax.optimization_barrier((key_value_weight, token))
    (base,) = call(
        "base",
        functools.partial(base_kernel, pool, parts, count, half),
        (*operands, jnp.transpose(weight, (1, 0, 2)), marked),
        chunks_in + [VMEM, ANY],
        [struct((all_rows, kv_local * pair), F32)],
        work=2 * all_rows * part * kv_local * pair,
        moved=3 << 20,
    )

    ratio = pool // tensor
    mine = None
    for j in range(ratio):
        for m in range(parts - 1, tensor, parts):
            pairs = [
                (i * tensor + s, (s * ratio + ((i // tensor) ^ j)) * tensor + ((i % tensor) ^ m))
                for i in range(pool)
                for s in range(tensor)
            ]
            moved = lax.ppermute(shrink, ("pool", "tensor"), pairs).astype(F32)
            mine = moved if mine is None else mine + moved
    sums = [mine] + ([over_pair(mine)] if parts == 2 else [])
    expanded = call(
        "expand",
        functools.partial(expand_kernel, pool, parts),
        (*sums, slots, base, adapter_up_key, adapter_up_value),
        [VMEM] * (parts + 4),
        [struct((count, kv_local * pair), F32)] + [struct((count, kv_local * pair), BF16)] * (pool - 1) + [TOKEN],
        [pltpu.VMEM((all_rows, LANES), F32)],
        work=4 * all_rows * LANES * up_here * LANES,
    )
    received = [None] * pool
    for k in range(pool - 1, 0, -1):
        received[k] = over_pool(expanded[k], k)
    acc, stat = call(
        "cached",
        cache_kernel,
        (packed[-1], queries, stored, expanded[pool]),
        [VMEM] * 3 + [ANY],
        [struct((count * heads, n), F32) for n in (size, LANES)],
        [pltpu.VMEM((count * heads, cache.shape[1]), t) for t in (F32, BF16)],
        work=4 * count * heads * cache.shape[1] * kv_local * size,
        moved=cache.size * 2,
    )
    return tuple(call(
        "finish",
        functools.partial(finish_kernel, pool),
        (expanded[0], *[received[k] for k in [pool - 1, *range(1, pool - 1)]], queries, acc, stat),
        [VMEM] * (pool + 3),
        [struct((rows, steps_new, heads * size), BF16), struct((rows, steps_new, kv_local, pair), BF16)],
        [pltpu.VMEM((count * heads, size), F32)],
        work=4 * count * heads * size * LANES,
    ))


def solution(mesh):
    return jax.shard_map(
        body,
        mesh=mesh,
        in_specs=(
            P(("groups", "pool"), None, None),
            P(("groups", "pool"), None, "tensor", None),
            P(("groups", "pool"), None, "tensor", None),
            P("pool", "tensor", None),
            P("tensor", "pool", None),
            P("pool", None, "tensor", None),
            P("pool", None, "tensor", None),
            P(("groups", "pool")),
            P(),
            P(("groups", "pool")),
        ),
        out_specs=(
            P(("groups", "pool"), None, "tensor"),
            P(("groups", "pool"), None, "tensor", None),
        ),
        check_vma=False,
    )
```

```python
import functools
import jax
import jax.numpy as jnp
from jax import lax
from jax.experimental import pallas as pl
from jax.experimental.pallas import tpu as pltpu
from jax.sharding import PartitionSpec as P

ADAPTER_SCALE = 0.5
LANES = 128
F32 = jnp.float32
BF16 = jnp.bfloat16
VMEM = pl.BlockSpec(memory_space=pltpu.VMEM)
SMEM = pl.BlockSpec(memory_space=pltpu.SMEM)
HBM = pl.BlockSpec(memory_space=pltpu.HBM)
ANY = pl.BlockSpec(memory_space=pl.ANY)
LIMIT = 16 * 1024 * 1024
WHOLE = (0, 1)
TAIL = 16
TOKEN = jax.ShapeDtypeStruct((8, LANES), F32)
PACK = 62 * 1024 * 1024


def dot(a, b):
    return jnp.dot(a, b, preferred_element_type=F32)


def dot_t(a, b):
    return lax.dot_general(a, b, (((1,), (1,)), ((), ())), preferred_element_type=F32)


def struct(shape, dtype):
    return jax.ShapeDtypeStruct(shape, dtype)


def cost(flops, moved):
    return pl.CostEstimate(flops=int(flops), bytes_accessed=int(moved), transcendentals=0)


def pack_kernel(pool, parts, request_adapter, adapter_storage, lengths, hidden, *refs):
    outs, (spans, pieces, ids, table, sizes, sems) = refs[:pool], refs[pool:]
    rows, steps_new, width = hidden.shape
    count = rows * steps_new
    part = width // pool
    half = part // parts
    me, side = lax.axis_index("pool"), lax.axis_index("tensor") % parts
    copies = [
        pltpu.make_async_copy(request_adapter, ids, sems.at[0]),
        pltpu.make_async_copy(adapter_storage, table, sems.at[1]),
        pltpu.make_async_copy(lengths, sizes, sems.at[2]),
    ]
    places = []
    for k in reversed(range(pool)):
        for i in range(parts if k in WHOLE else 1):
            start = (me ^ k) * part + (side if i == 0 else 1 - side) * half
            source = hidden.at[:, :, pl.ds(pl.multiple_of(start, LANES), half)]
            copies.append(pltpu.make_async_copy(source, pieces.at[len(places)], sems.at[3 + len(places)]))
            places.append((k, i * half // LANES))
    for c in copies:
        c.start()
    for c in copies[:3]:
        c.wait()
    lane = lax.broadcasted_iota(jnp.int32, (TAIL, LANES), 1) // steps_new
    slots = jnp.zeros((TAIL, LANES), jnp.int32)
    for r in range(rows):
        slots = jnp.where(lane == r, table[ids[r]], slots)
    slots = slots.astype(F32).astype(BF16)
    request = lax.broadcasted_iota(jnp.int32, spans.shape, 0)
    reach = jnp.zeros(spans.shape, jnp.int32)
    for r in range(rows):
        reach = jnp.where(request == r, sizes[r], reach)
    spans[...] = reach
    for k in range(pool):
        outs[k][-TAIL:, :] = slots
    for n, (k, first) in enumerate(places):
        copies[3 + n].wait()
        piece = pieces[n].reshape(count, half)
        for j in range(half // LANES):
            outs[k][(first + j) * count:(first + j + 1) * count, :] = piece[:, j * LANES:(j + 1) * LANES]


def both_sides(pool, parts, count, half, refs):
    side = lax.axis_index("tensor") % parts
    tiles = half // LANES

    def rows(chunk, first):
        return jnp.concatenate([chunk[j * count:(j + 1) * count, :] for j in range(first, first + tiles)], axis=1)

    sides = [(side * half, jnp.concatenate([rows(c, 0) for c in refs[:pool]], axis=0))]
    if parts == 2:
        swapped = iter(refs[pool:])
        rest = [rows(refs[k], tiles) if k in WHOLE else rows(next(swapped), 0) for k in range(pool)]
        sides.append(((1 - side) * half, jnp.concatenate(rest, axis=0)))
    return [(pl.ds(pl.multiple_of(start, half), half), x) for start, x in sides]


def shrink_kernel(pool, parts, count, half, *refs):
    down, shrink, slots_out, token = refs[-4:]
    token[...] = jnp.zeros_like(token)
    me = lax.axis_index("pool")
    first_slot = lax.axis_index("tensor") * down.shape[0]
    sides = both_sides(pool, parts, count, half, refs[:-4])
    row = lax.broadcasted_iota(jnp.int32, (count, LANES), 0)
    lane = lax.broadcasted_iota(jnp.int32, (count, LANES), 1)
    slots = []
    for c in refs[:pool]:
        line = c[-TAIL:, :].astype(F32)[:1, :]
        slots.append(jnp.sum(jnp.where(row == lane, line, 0.0), axis=1, keepdims=True))
    slots = jnp.broadcast_to(jnp.concatenate(slots, axis=0), (count * pool, LANES))
    slots_out[...] = slots
    step = 2 if down.shape[0] % 2 == 0 else 1
    total = jnp.zeros((count * pool, LANES), F32)
    for a in range(0, down.shape[0], step):
        out = 0.0
        for at, x in sides:
            out += dot(x, jnp.concatenate([down[a + i, at, :] for i in range(step)], axis=1))
        for i in range(step):
            match = slots == (first_slot + a + i).astype(F32)
            total = jnp.where(match, out[:, i * LANES:(i + 1) * LANES], total)
    total = total.astype(BF16)
    for k in range(pool):
        at = pl.ds(pl.multiple_of((me ^ k) * count, count), count)
        shrink[at, :] = total[k * count:(k + 1) * count]


def base_kernel(pool, parts, count, half, *refs):
    weight, up_key, up_value, _, base, key_table, value_table, token = refs[-8:]
    token[...] = jnp.zeros_like(token)
    sides = both_sides(pool, parts, count, half, refs[:-8])
    holders, rank, kv_local, size = up_key.shape
    for a in range(holders):
        at = slice(a * rank * kv_local, (a + 1) * rank * kv_local)
        key_table[at, :] = up_key[a].reshape(rank * kv_local, size)
        value_table[at, :] = up_value[a].reshape(rank * kv_local, size)
    for k in range(weight.shape[0]):
        out = 0.0
        for at, x in sides:
            out += dot(x, weight[k, at, :])
        base[:, k * weight.shape[2]:(k + 1) * weight.shape[2]] = out


def expand_kernel(pool, parts, rank, kv_local, *refs):
    sums, refs = refs[:parts], refs[parts:]
    slots_in, base = refs[:2]
    tables, (outs, token, scratch) = refs[2:4], (refs[4:4 + pool], refs[4 + pool], refs[5 + pool])
    token[...] = jnp.zeros_like(token)
    count = base.shape[0] // pool
    deep, size = rank * kv_local, tables[0].shape[1]
    holders = tables[0].shape[0] // deep
    me = lax.axis_index("pool")
    first_slot = me * holders
    total = sums[0][...]
    for s in sums[1:]:
        total = total + s[...]
    scratch[...] = total
    ordered = jnp.concatenate(
        [scratch[pl.ds(pl.multiple_of((me ^ k) * count, count), count), :] for k in range(pool)], axis=0
    ).astype(BF16)
    slots = jnp.concatenate([slots_in[:, :deep]] * kv_local, axis=0)
    row = lax.broadcasted_iota(jnp.int32, (2 * rank, deep), 0)
    col = lax.broadcasted_iota(jnp.int32, (2 * rank, deep), 1)
    for which, table in enumerate(tables):
        wide = []
        for k in range(kv_local):
            pick = (row == which * rank + col // kv_local) & (col % kv_local == k)
            wide.append(dot(ordered, pick.astype(F32).astype(BF16)))
        wide = jnp.concatenate(wide, axis=0)
        spread = [
            jnp.where(slots == (first_slot + a).astype(F32), wide, 0.0).astype(BF16) for a in range(holders)
        ]
        delta = dot(jnp.concatenate(spread, axis=1), table[...])
        for k in range(kv_local):
            at = slice((2 * k + which) * size, (2 * k + which + 1) * size)
            value = base[:, at] + ADAPTER_SCALE * delta[k * base.shape[0]:(k + 1) * base.shape[0]]
            outs[0][:, at] = value[:count]
            for j in range(1, pool):
                outs[j][:, at] = value[j * count:(j + 1) * count].astype(BF16)


def cache_kernel(spans, queries, cache, _, acc_out, top_out, total_out, bias_out, scores_all, weights_all):
    rows, steps_new, heads, size = queries.shape
    kv_local, depth = cache.shape[1:3]
    count = steps_new * heads
    which = lax.broadcasted_iota(jnp.int32, (count, 1), 0) % heads // (heads // kv_local)
    col = lax.broadcasted_iota(jnp.int32, (1, depth), 1)
    for r in range(rows):
        q = queries[r].reshape(count, size)
        scores = dot_t(q, cache[r, 0, :, :size])
        for k in range(1, kv_local):
            scores = jnp.where(which == k, dot_t(q, cache[r, k, :, :size]), scores)
        scores = jnp.where(col < spans[r:r + 1, :], scores * size ** -0.5, -1e30)
        scores_all[r * count:(r + 1) * count, :] = scores
    scores = scores_all[...]
    top = jnp.max(scores, axis=1, keepdims=True)
    weights = jnp.exp(scores - top)
    total = jnp.sum(weights, axis=1, keepdims=True)
    top_out[...] = jnp.broadcast_to(top, top_out.shape)
    total_out[...] = jnp.broadcast_to(total, total_out.shape)
    fresh = rows * steps_new
    column = lax.broadcasted_iota(jnp.int32, bias_out.shape, 1)
    line = lax.broadcasted_iota(jnp.int32, bias_out.shape, 0)
    token, other = line // heads, column % fresh
    valid = (
        (token // steps_new == other // steps_new)
        & (other <= token)
        & (line % heads // (heads // kv_local) == column // fresh)
    )
    bias_out[...] = jnp.where(valid, 0.0, -1e30)
    weights_all[...] = weights.astype(BF16)
    for r in range(rows):
        weights = weights_all[r * count:(r + 1) * count, :]
        mixed = dot(weights, cache[r, 0, :, size:])
        for k in range(1, kv_local):
            mixed = jnp.where(which == k, dot(weights, cache[r, k, :, size:]), mixed)
        acc_out[r * count:(r + 1) * count, :] = mixed


def finish_kernel(pool, own, *refs):
    parts, refs = refs[:pool - 1], refs[pool - 1:]
    queries, acc, top_before, total_before, bias, attended, fresh_out, scratch = refs
    rows, steps_new, heads, size = queries.shape
    count = rows * steps_new
    kv_local = own.shape[1] // (2 * size)
    total = own[...]
    for part in parts:
        total = total + part[...].astype(F32)
    fresh = total.astype(BF16)
    wide = 2 * size
    fresh_out[...] = jnp.stack([fresh[:, k * wide:(k + 1) * wide] for k in range(kv_local)], axis=1).reshape(fresh_out.shape)
    keys = jnp.concatenate([fresh[:, 2 * k * size:(2 * k + 1) * size] for k in range(kv_local)], axis=0)
    values = jnp.concatenate([fresh[:, (2 * k + 1) * size:(2 * k + 2) * size] for k in range(kv_local)], axis=0)
    scores = dot_t(queries[...].reshape(count * heads, size), keys) * size ** -0.5 + bias[...]
    top = jnp.maximum(top_before[...], jnp.max(scores, axis=1, keepdims=True))
    weights = jnp.exp(scores - top[:, :scores.shape[1]])
    keep = jnp.exp(top_before[...] - top)
    norm = 1.0 / (total_before[...] * keep + jnp.sum(weights, axis=1, keepdims=True))
    scratch[...] = (acc[...] * keep + dot(weights.astype(BF16), values)) * norm
    for h in range(heads):
        out = scratch[pl.ds(h, count, stride=heads), :].astype(BF16)
        attended[:, :, h * size:(h + 1) * size] = out.reshape(rows, steps_new, size)


def body(
    hidden,
    queries,
    cache,
    key_value_weight,
    adapter_down_weight,
    adapter_up_key,
    adapter_up_value,
    request_adapter,
    adapter_storage,
    lengths,
):
    pool, tensor = lax.axis_size("pool"), lax.axis_size("tensor")
    rows, steps_new, width = hidden.shape
    count = rows * steps_new
    part = width // pool
    down_here, up_here = adapter_down_weight.shape[0], adapter_up_key.shape[0]
    _, kv_local, pair = key_value_weight.shape
    heads, size = queries.shape[2:]
    assert adapter_storage.shape[0] <= 256 and count <= LANES and pool & (pool - 1) == 0 and tensor & (tensor - 1) == 0
    assert pool % tensor == 0 and down_here == up_here * (pool // tensor)
    parts = 2 if tensor % 2 == 0 else 1
    half = part // parts

    def over_pool(x, k):
        return lax.ppermute(x, "pool", [(i, i ^ k) for i in range(pool)])

    def over_pair(x):
        return lax.ppermute(x, "tensor", [(i, i ^ 1) for i in range(tensor)])

    def call(name, kernel, operands, in_specs, outs, scratch=(), work=0, moved=1 << 20, limit=LIMIT):
        return pl.pallas_call(
            kernel,
            out_shape=outs,
            in_specs=in_specs,
            out_specs=[VMEM] * len(outs),
            scratch_shapes=scratch,
            name=name,
            compiler_params=pltpu.CompilerParams(vmem_limit_bytes=limit),
            cost_estimate=cost(work, moved),
        )(*operands)

    chunks = [
        struct((count * (part if k in WHOLE else half) // LANES + TAIL, LANES), BF16) for k in range(pool)
    ]
    pieces = sum(parts if k in WHOLE else 1 for k in range(pool))
    packed = call(
        "pack",
        functools.partial(pack_kernel, pool, parts),
        tuple(pltpu.with_memory_space_constraint(x, pltpu.HBM) for x in (request_adapter, adapter_storage, lengths, hidden)),
        [HBM] * 4,
        chunks + [struct((rows, cache.shape[1]), jnp.int32)],
        [
            pltpu.VMEM((pieces, rows, steps_new, half), BF16),
            pltpu.SMEM(request_adapter.shape, jnp.int32),
            pltpu.SMEM(adapter_storage.shape, jnp.int32),
            pltpu.SMEM(lengths.shape, jnp.int32),
            pltpu.SemaphoreType.DMA((3 + pieces,)),
        ],
    )
    operands = [packed[0]] + [None] * (pool - 1)
    for k in range(pool - 1, 0, -1):
        operands[k] = over_pool(packed[k], k)
    stored, _ = lax.optimization_barrier((cache, packed[0]))
    stored = jnp.transpose(stored, (0, 2, 1, 3))
    swapped = {}
    for k in [*range(2, pool), 1]:
        operands[k], stored = lax.optimization_barrier((operands[k], stored))
        if parts == 2 and k not in WHOLE:
            swapped[k] = over_pair(operands[k])
    operands += [swapped[k] for k in sorted(swapped)]

    all_rows = pool * count
    chunks_in = [VMEM] * len(operands)
    shrink, slots, token = call(
        "shrink",
        functools.partial(shrink_kernel, pool, parts, count, half),
        (*operands, adapter_down_weight),
        chunks_in + [VMEM],
        [struct((all_rows, LANES), BF16), struct((all_rows, LANES), F32), TOKEN],
        work=2 * all_rows * part * down_here * LANES,
        moved=4 << 20,
    )
    weight, marked = lax.optimization_barrier((key_value_weight, token))
    _, rank, _, size = adapter_up_key.shape
    table = struct((up_here * rank * kv_local, size), BF16)
    base, key_table, value_table, token = call(
        "base",
        functools.partial(base_kernel, pool, parts, count, half),
        (*operands, jnp.transpose(weight, (1, 0, 2)), adapter_up_key, adapter_up_value, marked),
        chunks_in + [VMEM] * 3 + [ANY],
        [struct((all_rows, kv_local * pair), F32), table, table, TOKEN],
        work=2 * all_rows * part * kv_local * pair,
        moved=3 << 20,
    )

    ratio = pool // tensor
    mine = None
    for j in range(ratio):
        for m in range(parts - 1, tensor, parts):
            pairs = [
                (i * tensor + s, (s * ratio + ((i // tensor) ^ j)) * tensor + ((i % tensor) ^ m))
                for i in range(pool)
                for s in range(tensor)
            ]
            moved = lax.ppermute(shrink, ("pool", "tensor"), pairs).astype(F32)
            mine = moved if mine is None else mine + moved
    mine = mine + token[:1]
    sums = [mine] + ([over_pair(mine)] if parts == 2 else [])
    expanded = call(
        "expand",
        functools.partial(expand_kernel, pool, parts, rank, kv_local),
        (*sums, slots, base, key_table, value_table),
        [VMEM] * (parts + 4),
        [struct((count, kv_local * pair), F32)] + [struct((count, kv_local * pair), BF16)] * (pool - 1) + [TOKEN],
        [pltpu.VMEM((all_rows, LANES), F32)],
        work=4 * all_rows * LANES * up_here * LANES,
    )
    received = [None] * pool
    for k in range(pool - 1, 0, -1):
        received[k] = over_pool(expanded[k], k)
    acc, top, total, bias = call(
        "cached",
        cache_kernel,
        (packed[-1], queries, stored, expanded[pool]),
        [VMEM] * 3 + [ANY],
        [struct((count * heads, n), F32) for n in (size, size, size, count * kv_local)],
        [pltpu.VMEM((count * heads, cache.shape[1]), t) for t in (F32, BF16)],
        work=4 * count * heads * cache.shape[1] * kv_local * size,
        moved=cache.size * 2,
    )
    return tuple(call(
        "finish",
        functools.partial(finish_kernel, pool),
        (expanded[0], *[received[k] for k in [2, 1, *range(3, pool)]], queries, acc, top, total, bias),
        [VMEM] * (pool + 5),
        [struct((rows, steps_new, heads * size), BF16), struct((rows, steps_new, kv_local, pair), BF16)],
        [pltpu.VMEM((count * heads, size), F32)],
        work=4 * count * heads * size * LANES,
    ))


def solution(mesh):
    return jax.shard_map(
        body,
        mesh=mesh,
        in_specs=(
            P(("groups", "pool"), None, None),
            P(("groups", "pool"), None, "tensor", None),
            P(("groups", "pool"), None, "tensor", None),
            P("pool", "tensor", None),
            P("tensor", "pool", None),
            P("pool", None, "tensor", None),
            P("pool", None, "tensor", None),
            P(("groups", "pool")),
            P(),
            P(("groups", "pool")),
        ),
        out_specs=(
            P(("groups", "pool"), None, "tensor"),
            P(("groups", "pool"), None, "tensor", None),
        ),
        check_vma=False,
    )
```

```python
import functools
import jax
import jax.numpy as jnp
from jax import lax
from jax.experimental import pallas as pl
from jax.experimental.pallas import tpu as pltpu
from jax.sharding import PartitionSpec as P

ADAPTER_SCALE = 0.5
LANES = 128
F32 = jnp.float32
BF16 = jnp.bfloat16
VMEM = pl.BlockSpec(memory_space=pltpu.VMEM)
SMEM = pl.BlockSpec(memory_space=pltpu.SMEM)
HBM = pl.BlockSpec(memory_space=pltpu.HBM)
ANY = pl.BlockSpec(memory_space=pl.ANY)
LIMIT = 16 * 1024 * 1024
WHOLE = (0, 1)
TAIL = 16
TOKEN = jax.ShapeDtypeStruct((8, LANES), F32)
PACK = 62 * 1024 * 1024


def dot(a, b):
    return jnp.dot(a, b, preferred_element_type=F32)


def dot_t(a, b):
    return lax.dot_general(a, b, (((1,), (1,)), ((), ())), preferred_element_type=F32)


def struct(shape, dtype):
    return jax.ShapeDtypeStruct(shape, dtype)


def cost(flops, moved):
    return pl.CostEstimate(flops=int(flops), bytes_accessed=int(moved), transcendentals=0)


def pack_kernel(pool, parts, request_adapter, adapter_storage, lengths, hidden, *refs):
    outs, (spans, pieces, ids, table, sizes, sems) = refs[:pool], refs[pool:]
    rows, steps_new, width = hidden.shape
    count = rows * steps_new
    part = width // pool
    half = part // parts
    me, side = lax.axis_index("pool"), lax.axis_index("tensor") % parts
    copies = [
        pltpu.make_async_copy(request_adapter, ids, sems.at[0]),
        pltpu.make_async_copy(adapter_storage, table, sems.at[1]),
        pltpu.make_async_copy(lengths, sizes, sems.at[2]),
    ]
    places = []
    for k in reversed(range(pool)):
        for i in range(parts if k in WHOLE else 1):
            start = (me ^ k) * part + (side if i == 0 else 1 - side) * half
            source = hidden.at[:, :, pl.ds(pl.multiple_of(start, LANES), half)]
            copies.append(pltpu.make_async_copy(source, pieces.at[len(places)], sems.at[3 + len(places)]))
            places.append((k, i * half // LANES))
    for c in copies:
        c.start()
    for c in copies[:3]:
        c.wait()
    lane = lax.broadcasted_iota(jnp.int32, (TAIL, LANES), 1) // steps_new
    slots = jnp.zeros((TAIL, LANES), jnp.int32)
    for r in range(rows):
        slots = jnp.where(lane == r, table[ids[r]], slots)
    slots = slots.astype(F32).astype(BF16)
    request = lax.broadcasted_iota(jnp.int32, spans.shape, 0)
    reach = jnp.zeros(spans.shape, jnp.int32)
    for r in range(rows):
        reach = jnp.where(request == r, sizes[r], reach)
    spans[...] = reach
    for k in range(pool):
        outs[k][-TAIL:, :] = slots
    for n, (k, first) in enumerate(places):
        copies[3 + n].wait()
        piece = pieces[n].reshape(count, half)
        for j in range(half // LANES):
            outs[k][(first + j) * count:(first + j + 1) * count, :] = piece[:, j * LANES:(j + 1) * LANES]


def both_sides(pool, parts, count, half, refs):
    side = lax.axis_index("tensor") % parts
    tiles = half // LANES

    def rows(chunk, first):
        return jnp.concatenate([chunk[j * count:(j + 1) * count, :] for j in range(first, first + tiles)], axis=1)

    sides = [(side * half, jnp.concatenate([rows(c, 0) for c in refs[:pool]], axis=0))]
    if parts == 2:
        swapped = iter(refs[pool:])
        rest = [rows(refs[k], tiles) if k in WHOLE else rows(next(swapped), 0) for k in range(pool)]
        sides.append(((1 - side) * half, jnp.concatenate(rest, axis=0)))
    return [(pl.ds(pl.multiple_of(start, half), half), x) for start, x in sides]


def shrink_kernel(pool, parts, count, half, *refs):
    down, shrink, slots_out, token = refs[-4:]
    token[...] = jnp.zeros_like(token)
    me = lax.axis_index("pool")
    first_slot = lax.axis_index("tensor") * down.shape[0]
    sides = both_sides(pool, parts, count, half, refs[:-4])
    row = lax.broadcasted_iota(jnp.int32, (count, LANES), 0)
    lane = lax.broadcasted_iota(jnp.int32, (count, LANES), 1)
    slots = []
    for c in refs[:pool]:
        line = c[-TAIL:, :].astype(F32)[:1, :]
        slots.append(jnp.sum(jnp.where(row == lane, line, 0.0), axis=1, keepdims=True))
    slots = jnp.broadcast_to(jnp.concatenate(slots, axis=0), (count * pool, LANES))
    slots_out[...] = slots
    step = 2 if down.shape[0] % 2 == 0 else 1
    total = jnp.zeros((count * pool, LANES), F32)
    for a in range(0, down.shape[0], step):
        out = 0.0
        for at, x in sides:
            out += dot(x, jnp.concatenate([down[a + i, at, :] for i in range(step)], axis=1))
        for i in range(step):
            match = slots == (first_slot + a + i).astype(F32)
            total = jnp.where(match, out[:, i * LANES:(i + 1) * LANES], total)
    total = total.astype(BF16)
    for k in range(pool):
        at = pl.ds(pl.multiple_of((me ^ k) * count, count), count)
        shrink[at, :] = total[k * count:(k + 1) * count]


def base_kernel(pool, parts, count, half, *refs):
    weight, up_key, up_value, _, base, table, token = refs[-7:]
    token[...] = jnp.zeros_like(token)
    sides = both_sides(pool, parts, count, half, refs[:-7])
    holders, rank, kv_local, size = up_key.shape
    row = lax.broadcasted_iota(jnp.int32, (kv_local * rank, rank * kv_local), 0)
    col = lax.broadcasted_iota(jnp.int32, (kv_local * rank, rank * kv_local), 1)
    pick = (row // rank == col % kv_local) & (row % rank == col // kv_local)
    pick = pick.astype(F32).astype(BF16)
    nothing = jnp.zeros((rank, size), BF16)
    for a in range(holders):
        for which, up in enumerate((up_key, up_value)):
            heads = dot(pick, up[a].reshape(rank * kv_local, size)).astype(BF16)
            at = slice((2 * a + which) * rank, (2 * a + which + 1) * rank)
            for k in range(kv_local):
                for i in range(2):
                    value = heads[k * rank:(k + 1) * rank] if i == which else nothing
                    table[at, (2 * k + i) * size:(2 * k + i + 1) * size] = value
    for k in range(weight.shape[0]):
        out = 0.0
        for at, x in sides:
            out += dot(x, weight[k, at, :])
        base[:, k * weight.shape[2]:(k + 1) * weight.shape[2]] = out


def expand_kernel(pool, parts, *refs):
    sums, (slots_in, base, table), refs = refs[:parts], refs[parts:parts + 3], refs[parts + 3:]
    outs, token, scratch = refs[:pool], refs[pool], refs[pool + 1]
    token[...] = jnp.zeros_like(token)
    count, wide = base.shape[0] // pool, slots_in.shape[1]
    holders = table.shape[0] // wide
    me = lax.axis_index("pool")
    total = sums[0][...]
    for s in sums[1:]:
        total = total + s[...]
    scratch[...] = total
    ordered = jnp.concatenate(
        [scratch[pl.ds(pl.multiple_of((me ^ k) * count, count), count), :] for k in range(pool)], axis=0
    )
    slots = slots_in[...] - (me * holders).astype(F32)
    spread = [jnp.where(slots == float(a), ordered, 0.0).astype(BF16) for a in range(holders)]
    value = base[...] + ADAPTER_SCALE * dot(jnp.concatenate(spread, axis=1), table[...])
    outs[0][...] = value[:count]
    for j in range(1, pool):
        outs[j][...] = value[j * count:(j + 1) * count].astype(BF16)


def cache_kernel(spans, queries, cache, _, acc_out, top_out, total_out, bias_out, scores_all, weights_all):
    rows, steps_new, heads, size = queries.shape
    kv_local, depth = cache.shape[1:3]
    count = steps_new * heads
    which = lax.broadcasted_iota(jnp.int32, (count, 1), 0) % heads // (heads // kv_local)
    col = lax.broadcasted_iota(jnp.int32, (1, depth), 1)
    for r in range(rows):
        q = queries[r].reshape(count, size)
        scores = dot_t(q, cache[r, 0, :, :size])
        for k in range(1, kv_local):
            scores = jnp.where(which == k, dot_t(q, cache[r, k, :, :size]), scores)
        scores = jnp.where(col < spans[r:r + 1, :], scores * size ** -0.5, -1e30)
        scores_all[r * count:(r + 1) * count, :] = scores
    scores = scores_all[...]
    top = jnp.max(scores, axis=1, keepdims=True)
    weights = jnp.exp(scores - top)
    total = jnp.sum(weights, axis=1, keepdims=True)
    top_out[...] = jnp.broadcast_to(top, top_out.shape)
    total_out[...] = jnp.broadcast_to(total, total_out.shape)
    fresh = rows * steps_new
    column = lax.broadcasted_iota(jnp.int32, bias_out.shape, 1)
    line = lax.broadcasted_iota(jnp.int32, bias_out.shape, 0)
    token, other = line // heads, column % fresh
    valid = (
        (token // steps_new == other // steps_new)
        & (other <= token)
        & (line % heads // (heads // kv_local) == column // fresh)
    )
    bias_out[...] = jnp.where(valid, 0.0, -1e30)
    weights_all[...] = weights.astype(BF16)
    for r in range(rows):
        weights = weights_all[r * count:(r + 1) * count, :]
        mixed = dot(weights, cache[r, 0, :, size:])
        for k in range(1, kv_local):
            mixed = jnp.where(which == k, dot(weights, cache[r, k, :, size:]), mixed)
        acc_out[r * count:(r + 1) * count, :] = mixed


def finish_kernel(pool, own, *refs):
    parts, refs = refs[:pool - 1], refs[pool - 1:]
    queries, acc, top_before, total_before, bias, attended, fresh_out, scratch = refs
    rows, steps_new, heads, size = queries.shape
    count = rows * steps_new
    kv_local = own.shape[1] // (2 * size)
    total = own[...]
    for part in parts:
        total = total + part[...].astype(F32)
    fresh = total.astype(BF16)
    wide = 2 * size
    fresh_out[...] = jnp.stack([fresh[:, k * wide:(k + 1) * wide] for k in range(kv_local)], axis=1).reshape(fresh_out.shape)
    keys = jnp.concatenate([fresh[:, 2 * k * size:(2 * k + 1) * size] for k in range(kv_local)], axis=0)
    values = jnp.concatenate([fresh[:, (2 * k + 1) * size:(2 * k + 2) * size] for k in range(kv_local)], axis=0)
    scores = dot_t(queries[...].reshape(count * heads, size), keys) * size ** -0.5 + bias[...]
    top = jnp.maximum(top_before[...], jnp.max(scores, axis=1, keepdims=True))
    weights = jnp.exp(scores - top[:, :scores.shape[1]])
    keep = jnp.exp(top_before[...] - top)
    norm = 1.0 / (total_before[...] * keep + jnp.sum(weights, axis=1, keepdims=True))
    scratch[...] = (acc[...] * keep + dot(weights.astype(BF16), values)) * norm
    for h in range(heads):
        out = scratch[pl.ds(h, count, stride=heads), :].astype(BF16)
        attended[:, :, h * size:(h + 1) * size] = out.reshape(rows, steps_new, size)


def body(
    hidden,
    queries,
    cache,
    key_value_weight,
    adapter_down_weight,
    adapter_up_key,
    adapter_up_value,
    request_adapter,
    adapter_storage,
    lengths,
):
    pool, tensor = lax.axis_size("pool"), lax.axis_size("tensor")
    rows, steps_new, width = hidden.shape
    count = rows * steps_new
    part = width // pool
    down_here, up_here = adapter_down_weight.shape[0], adapter_up_key.shape[0]
    _, kv_local, pair = key_value_weight.shape
    heads, size = queries.shape[2:]
    assert adapter_storage.shape[0] <= 256 and count <= LANES and pool & (pool - 1) == 0 and tensor & (tensor - 1) == 0
    assert pool % tensor == 0 and down_here == up_here * (pool // tensor)
    parts = 2 if tensor % 2 == 0 else 1
    half = part // parts

    def over_pool(x, k):
        return lax.ppermute(x, "pool", [(i, i ^ k) for i in range(pool)])

    def over_pair(x):
        return lax.ppermute(x, "tensor", [(i, i ^ 1) for i in range(tensor)])

    def call(name, kernel, operands, in_specs, outs, scratch=(), work=0, moved=1 << 20, limit=LIMIT):
        return pl.pallas_call(
            kernel,
            out_shape=outs,
            in_specs=in_specs,
            out_specs=[VMEM] * len(outs),
            scratch_shapes=scratch,
            name=name,
            compiler_params=pltpu.CompilerParams(vmem_limit_bytes=limit),
            cost_estimate=cost(work, moved),
        )(*operands)

    chunks = [
        struct((count * (part if k in WHOLE else half) // LANES + TAIL, LANES), BF16) for k in range(pool)
    ]
    pieces = sum(parts if k in WHOLE else 1 for k in range(pool))
    packed = call(
        "pack",
        functools.partial(pack_kernel, pool, parts),
        tuple(pltpu.with_memory_space_constraint(x, pltpu.HBM) for x in (request_adapter, adapter_storage, lengths, hidden)),
        [HBM] * 4,
        chunks + [struct((rows, cache.shape[1]), jnp.int32)],
        [
            pltpu.VMEM((pieces, rows, steps_new, half), BF16),
            pltpu.SMEM(request_adapter.shape, jnp.int32),
            pltpu.SMEM(adapter_storage.shape, jnp.int32),
            pltpu.SMEM(lengths.shape, jnp.int32),
            pltpu.SemaphoreType.DMA((3 + pieces,)),
        ],
    )
    operands = [packed[0]] + [None] * (pool - 1)
    for k in range(pool - 1, 0, -1):
        operands[k] = over_pool(packed[k], k)
    stored, _ = lax.optimization_barrier((cache, packed[0]))
    stored = jnp.transpose(stored, (0, 2, 1, 3))
    swapped = {}
    for k in [*range(2, pool), 1]:
        operands[k], stored = lax.optimization_barrier((operands[k], stored))
        if parts == 2 and k not in WHOLE:
            swapped[k] = over_pair(operands[k])
    operands += [swapped[k] for k in sorted(swapped)]

    all_rows = pool * count
    chunks_in = [VMEM] * len(operands)
    shrink, slots, token = call(
        "shrink",
        functools.partial(shrink_kernel, pool, parts, count, half),
        (*operands, adapter_down_weight),
        chunks_in + [VMEM],
        [struct((all_rows, LANES), BF16), struct((all_rows, LANES), F32), TOKEN],
        work=2 * all_rows * part * down_here * LANES,
        moved=4 << 20,
    )
    weight, marked = lax.optimization_barrier((key_value_weight, token))
    rank = adapter_up_key.shape[1]
    base, table, token = call(
        "base",
        functools.partial(base_kernel, pool, parts, count, half),
        (*operands, jnp.transpose(weight, (1, 0, 2)), adapter_up_key, adapter_up_value, marked),
        chunks_in + [VMEM] * 3 + [ANY],
        [
            struct((all_rows, kv_local * pair), F32),
            struct((up_here * 2 * rank, kv_local * pair), BF16),
            TOKEN,
        ],
        work=2 * all_rows * part * kv_local * pair,
        moved=3 << 20,
    )

    ratio = pool // tensor
    mine = None
    for j in range(ratio):
        for m in range(parts - 1, tensor, parts):
            pairs = [
                (i * tensor + s, (s * ratio + ((i // tensor) ^ j)) * tensor + ((i % tensor) ^ m))
                for i in range(pool)
                for s in range(tensor)
            ]
            moved = lax.ppermute(shrink, ("pool", "tensor"), pairs).astype(F32)
            mine = moved if mine is None else mine + moved
    mine = mine + token[:1]
    sums = [mine] + ([over_pair(mine)] if parts == 2 else [])
    expanded = call(
        "expand",
        functools.partial(expand_kernel, pool, parts),
        (*sums, slots, base, table),
        [VMEM] * (parts + 3),
        [struct((count, kv_local * pair), F32)] + [struct((count, kv_local * pair), BF16)] * (pool - 1) + [TOKEN],
        [pltpu.VMEM((all_rows, LANES), F32)],
        work=4 * all_rows * LANES * up_here * LANES,
    )
    received = [None] * pool
    for k in range(pool - 1, 0, -1):
        received[k] = over_pool(expanded[k], k)
    acc, top, total, bias = call(
        "cached",
        cache_kernel,
        (packed[-1], queries, stored, expanded[pool]),
        [VMEM] * 3 + [ANY],
        [struct((count * heads, n), F32) for n in (size, size, size, count * kv_local)],
        [pltpu.VMEM((count * heads, cache.shape[1]), t) for t in (F32, BF16)],
        work=4 * count * heads * cache.shape[1] * kv_local * size,
        moved=cache.size * 2,
    )
    return tuple(call(
        "finish",
        functools.partial(finish_kernel, pool),
        (expanded[0], *[received[k] for k in [2, 1, *range(3, pool)]], queries, acc, top, total, bias),
        [VMEM] * (pool + 5),
        [struct((rows, steps_new, heads * size), BF16), struct((rows, steps_new, kv_local, pair), BF16)],
        [pltpu.VMEM((count * heads, size), F32)],
        work=4 * count * heads * size * LANES,
    ))


def solution(mesh):
    return jax.shard_map(
        body,
        mesh=mesh,
        in_specs=(
            P(("groups", "pool"), None, None),
            P(("groups", "pool"), None, "tensor", None),
            P(("groups", "pool"), None, "tensor", None),
            P("pool", "tensor", None),
            P("tensor", "pool", None),
            P("pool", None, "tensor", None),
            P("pool", None, "tensor", None),
            P(("groups", "pool")),
            P(),
            P(("groups", "pool")),
        ),
        out_specs=(
            P(("groups", "pool"), None, "tensor"),
            P(("groups", "pool"), None, "tensor", None),
        ),
        check_vma=False,
    )
```

```python
import functools
import jax
import jax.numpy as jnp
from jax import lax
from jax.experimental import pallas as pl
from jax.experimental.pallas import tpu as pltpu
from jax.sharding import PartitionSpec as P

ADAPTER_SCALE = 0.5
LANES = 128
F32 = jnp.float32
BF16 = jnp.bfloat16
VMEM = pl.BlockSpec(memory_space=pltpu.VMEM)
SMEM = pl.BlockSpec(memory_space=pltpu.SMEM)
HBM = pl.BlockSpec(memory_space=pltpu.HBM)
ANY = pl.BlockSpec(memory_space=pl.ANY)
LIMIT = 16 * 1024 * 1024
WHOLE = (0, 1)
TAIL = 16
TOKEN = jax.ShapeDtypeStruct((8, LANES), F32)
PACK = 62 * 1024 * 1024


def dot(a, b):
    return jnp.dot(a, b, preferred_element_type=F32)


def dot_t(a, b):
    return lax.dot_general(a, b, (((1,), (1,)), ((), ())), preferred_element_type=F32)


def struct(shape, dtype):
    return jax.ShapeDtypeStruct(shape, dtype)


def cost(flops, moved):
    return pl.CostEstimate(flops=int(flops), bytes_accessed=int(moved), transcendentals=0)


def pack_kernel(pool, parts, request_adapter, adapter_storage, lengths, hidden, *refs):
    outs, (spans, pieces, ids, table, sizes, sems) = refs[:pool], refs[pool:]
    rows, steps_new, width = hidden.shape
    count = rows * steps_new
    part = width // pool
    half = part // parts
    me, side = lax.axis_index("pool"), lax.axis_index("tensor") % parts
    copies = [
        pltpu.make_async_copy(request_adapter, ids, sems.at[0]),
        pltpu.make_async_copy(adapter_storage, table, sems.at[1]),
        pltpu.make_async_copy(lengths, sizes, sems.at[2]),
    ]
    places = []
    for k in reversed(range(pool)):
        for i in range(parts if k in WHOLE else 1):
            start = (me ^ k) * part + (side if i == 0 else 1 - side) * half
            source = hidden.at[:, :, pl.ds(pl.multiple_of(start, LANES), half)]
            copies.append(pltpu.make_async_copy(source, pieces.at[len(places)], sems.at[3 + len(places)]))
            places.append((k, i * half // LANES))
    for c in copies:
        c.start()
    for c in copies[:3]:
        c.wait()
    lane = lax.broadcasted_iota(jnp.int32, (TAIL, LANES), 1) // steps_new
    slots = jnp.zeros((TAIL, LANES), jnp.int32)
    for r in range(rows):
        slots = jnp.where(lane == r, table[ids[r]], slots)
    slots = slots.astype(F32).astype(BF16)
    request = lax.broadcasted_iota(jnp.int32, spans.shape, 0)
    reach = jnp.zeros(spans.shape, jnp.int32)
    for r in range(rows):
        reach = jnp.where(request == r, sizes[r], reach)
    spans[...] = reach
    for k in range(pool):
        outs[k][-TAIL:, :] = slots
    for n, (k, first) in enumerate(places):
        copies[3 + n].wait()
        piece = pieces[n].reshape(count, half)
        for j in range(half // LANES):
            outs[k][(first + j) * count:(first + j + 1) * count, :] = piece[:, j * LANES:(j + 1) * LANES]


def both_sides(pool, parts, count, half, refs):
    side = lax.axis_index("tensor") % parts
    tiles = half // LANES

    def rows(chunk, first):
        return jnp.concatenate([chunk[j * count:(j + 1) * count, :] for j in range(first, first + tiles)], axis=1)

    sides = [(side * half, jnp.concatenate([rows(c, 0) for c in refs[:pool]], axis=0))]
    if parts == 2:
        swapped = iter(refs[pool:])
        rest = [rows(refs[k], tiles) if k in WHOLE else rows(next(swapped), 0) for k in range(pool)]
        sides.append(((1 - side) * half, jnp.concatenate(rest, axis=0)))
    return [(pl.ds(pl.multiple_of(start, half), half), x) for start, x in sides]


def shrink_kernel(pool, parts, count, half, *refs):
    down, shrink, slots_out, token = refs[-4:]
    token[...] = jnp.zeros_like(token)
    me = lax.axis_index("pool")
    first_slot = lax.axis_index("tensor") * down.shape[0]
    sides = both_sides(pool, parts, count, half, refs[:-4])
    row = lax.broadcasted_iota(jnp.int32, (count, LANES), 0)
    lane = lax.broadcasted_iota(jnp.int32, (count, LANES), 1)
    slots = []
    for c in refs[:pool]:
        line = c[-TAIL:, :].astype(F32)[:1, :]
        slots.append(jnp.sum(jnp.where(row == lane, line, 0.0), axis=1, keepdims=True))
    slots = jnp.broadcast_to(jnp.concatenate(slots, axis=0), (count * pool, LANES))
    slots_out[...] = slots
    step = 2 if down.shape[0] % 2 == 0 else 1
    total = jnp.zeros((count * pool, LANES), F32)
    for a in range(0, down.shape[0], step):
        out = 0.0
        for at, x in sides:
            out += dot(x, jnp.concatenate([down[a + i, at, :] for i in range(step)], axis=1))
        for i in range(step):
            match = slots == (first_slot + a + i).astype(F32)
            total = jnp.where(match, out[:, i * LANES:(i + 1) * LANES], total)
    total = total.astype(BF16)
    for k in range(pool):
        at = pl.ds(pl.multiple_of((me ^ k) * count, count), count)
        shrink[at, :] = total[k * count:(k + 1) * count]


def base_kernel(pool, parts, count, half, *refs):
    weight, up_key, up_value, _, base, table, token = refs[-7:]
    token[...] = jnp.zeros_like(token)
    sides = both_sides(pool, parts, count, half, refs[:-7])
    holders, rank, kv_local, size = up_key.shape
    row = lax.broadcasted_iota(jnp.int32, (kv_local * rank, rank * kv_local), 0)
    col = lax.broadcasted_iota(jnp.int32, (kv_local * rank, rank * kv_local), 1)
    pick = (row // rank == col % kv_local) & (row % rank == col // kv_local)
    pick = pick.astype(F32).astype(BF16)
    nothing = jnp.zeros((rank, size), BF16)
    for a in range(holders):
        for which, up in enumerate((up_key, up_value)):
            heads = dot(pick, up[a].reshape(rank * kv_local, size)).astype(BF16)
            at = slice((2 * a + which) * rank, (2 * a + which + 1) * rank)
            for k in range(kv_local):
                for i in range(2):
                    value = heads[k * rank:(k + 1) * rank] if i == which else nothing
                    table[at, (2 * k + i) * size:(2 * k + i + 1) * size] = value
    for k in range(weight.shape[0]):
        out = 0.0
        for at, x in sides:
            out += dot(x, weight[k, at, :])
        base[:, k * weight.shape[2]:(k + 1) * weight.shape[2]] = out


def expand_kernel(pool, parts, *refs):
    sums, (slots_in, base, table), refs = refs[:parts], refs[parts:parts + 3], refs[parts + 3:]
    outs, token, scratch, values = refs[:pool], *refs[pool:]
    token[...] = jnp.zeros_like(token)
    count, wide = base.shape[0] // pool, slots_in.shape[1]
    holders = table.shape[0] // wide
    me = lax.axis_index("pool")
    total = sums[0][...]
    for s in sums[1:]:
        total = total + s[...]
    scratch[...] = total
    ordered = jnp.concatenate(
        [scratch[pl.ds(pl.multiple_of((me ^ k) * count, count), count), :] for k in range(pool)], axis=0
    )
    slots = slots_in[...] - (me * holders).astype(F32)
    spread = [jnp.where(slots == float(a), ordered, 0.0).astype(BF16) for a in range(holders)]
    value = base[...] + ADAPTER_SCALE * dot(jnp.concatenate(spread, axis=1), table[...])
    outs[0][...] = value[:count]
    values[...] = value
    for j in range(1, pool):
        k = me ^ ((me + j) % pool)
        outs[j][...] = values[pl.ds(pl.multiple_of(k * count, count), count), :].astype(BF16)


def cache_kernel(spans, queries, cache, _, acc_out, top_out, total_out, bias_out, scores_all, weights_all):
    rows, steps_new, heads, size = queries.shape
    kv_local, depth = cache.shape[1:3]
    count = steps_new * heads
    which = lax.broadcasted_iota(jnp.int32, (count, 1), 0) % heads // (heads // kv_local)
    col = lax.broadcasted_iota(jnp.int32, (1, depth), 1)
    for r in range(rows):
        q = queries[r].reshape(count, size)
        scores = dot_t(q, cache[r, 0, :, :size])
        for k in range(1, kv_local):
            scores = jnp.where(which == k, dot_t(q, cache[r, k, :, :size]), scores)
        scores = jnp.where(col < spans[r:r + 1, :], scores * size ** -0.5, -1e30)
        scores_all[r * count:(r + 1) * count, :] = scores
    scores = scores_all[...]
    top = jnp.max(scores, axis=1, keepdims=True)
    weights = jnp.exp(scores - top)
    total = jnp.sum(weights, axis=1, keepdims=True)
    top_out[...] = jnp.broadcast_to(top, top_out.shape)
    total_out[...] = jnp.broadcast_to(total, total_out.shape)
    fresh = rows * steps_new
    column = lax.broadcasted_iota(jnp.int32, bias_out.shape, 1)
    line = lax.broadcasted_iota(jnp.int32, bias_out.shape, 0)
    token, other = line // heads, column % fresh
    valid = (
        (token // steps_new == other // steps_new)
        & (other <= token)
        & (line % heads // (heads // kv_local) == column // fresh)
    )
    bias_out[...] = jnp.where(valid, 0.0, -1e30)
    weights_all[...] = weights.astype(BF16)
    for r in range(rows):
        weights = weights_all[r * count:(r + 1) * count, :]
        mixed = dot(weights, cache[r, 0, :, size:])
        for k in range(1, kv_local):
            mixed = jnp.where(which == k, dot(weights, cache[r, k, :, size:]), mixed)
        acc_out[r * count:(r + 1) * count, :] = mixed


def finish_kernel(pool, own, *refs):
    parts, refs = refs[:pool - 1], refs[pool - 1:]
    queries, acc, top_before, total_before, bias, attended, fresh_out, scratch = refs
    rows, steps_new, heads, size = queries.shape
    count = rows * steps_new
    kv_local = own.shape[1] // (2 * size)
    total = own[...]
    for part in parts:
        total = total + part[...].astype(F32)
    fresh = total.astype(BF16)
    wide = 2 * size
    fresh_out[...] = jnp.stack([fresh[:, k * wide:(k + 1) * wide] for k in range(kv_local)], axis=1).reshape(fresh_out.shape)
    keys = jnp.concatenate([fresh[:, 2 * k * size:(2 * k + 1) * size] for k in range(kv_local)], axis=0)
    values = jnp.concatenate([fresh[:, (2 * k + 1) * size:(2 * k + 2) * size] for k in range(kv_local)], axis=0)
    scores = dot_t(queries[...].reshape(count * heads, size), keys) * size ** -0.5 + bias[...]
    top = jnp.maximum(top_before[...], jnp.max(scores, axis=1, keepdims=True))
    weights = jnp.exp(scores - top[:, :scores.shape[1]])
    keep = jnp.exp(top_before[...] - top)
    norm = 1.0 / (total_before[...] * keep + jnp.sum(weights, axis=1, keepdims=True))
    scratch[...] = (acc[...] * keep + dot(weights.astype(BF16), values)) * norm
    for h in range(heads):
        out = scratch[pl.ds(h, count, stride=heads), :].astype(BF16)
        attended[:, :, h * size:(h + 1) * size] = out.reshape(rows, steps_new, size)


def body(
    hidden,
    queries,
    cache,
    key_value_weight,
    adapter_down_weight,
    adapter_up_key,
    adapter_up_value,
    request_adapter,
    adapter_storage,
    lengths,
):
    pool, tensor = lax.axis_size("pool"), lax.axis_size("tensor")
    rows, steps_new, width = hidden.shape
    count = rows * steps_new
    part = width // pool
    down_here, up_here = adapter_down_weight.shape[0], adapter_up_key.shape[0]
    _, kv_local, pair = key_value_weight.shape
    heads, size = queries.shape[2:]
    assert adapter_storage.shape[0] <= 256 and count <= LANES and pool & (pool - 1) == 0 and tensor & (tensor - 1) == 0
    assert pool % tensor == 0 and down_here == up_here * (pool // tensor)
    parts = 2 if tensor % 2 == 0 else 1
    half = part // parts

    def over_pool(x, k):
        return lax.ppermute(x, "pool", [(i, i ^ k) for i in range(pool)])

    def over_pair(x):
        return lax.ppermute(x, "tensor", [(i, i ^ 1) for i in range(tensor)])

    def call(name, kernel, operands, in_specs, outs, scratch=(), work=0, moved=1 << 20, limit=LIMIT):
        return pl.pallas_call(
            kernel,
            out_shape=outs,
            in_specs=in_specs,
            out_specs=[VMEM] * len(outs),
            scratch_shapes=scratch,
            name=name,
            compiler_params=pltpu.CompilerParams(vmem_limit_bytes=limit),
            cost_estimate=cost(work, moved),
        )(*operands)

    chunks = [
        struct((count * (part if k in WHOLE else half) // LANES + TAIL, LANES), BF16) for k in range(pool)
    ]
    pieces = sum(parts if k in WHOLE else 1 for k in range(pool))
    packed = call(
        "pack",
        functools.partial(pack_kernel, pool, parts),
        tuple(pltpu.with_memory_space_constraint(x, pltpu.HBM) for x in (request_adapter, adapter_storage, lengths, hidden)),
        [HBM] * 4,
        chunks + [struct((rows, cache.shape[1]), jnp.int32)],
        [
            pltpu.VMEM((pieces, rows, steps_new, half), BF16),
            pltpu.SMEM(request_adapter.shape, jnp.int32),
            pltpu.SMEM(adapter_storage.shape, jnp.int32),
            pltpu.SMEM(lengths.shape, jnp.int32),
            pltpu.SemaphoreType.DMA((3 + pieces,)),
        ],
    )
    operands = [packed[0]] + [None] * (pool - 1)
    for k in range(pool - 1, 0, -1):
        operands[k] = over_pool(packed[k], k)
    stored, _ = lax.optimization_barrier((cache, packed[0]))
    stored = jnp.transpose(stored, (0, 2, 1, 3))
    swapped = {}
    for k in [*range(2, pool), 1]:
        operands[k], stored = lax.optimization_barrier((operands[k], stored))
        if parts == 2 and k not in WHOLE:
            swapped[k] = over_pair(operands[k])
    operands += [swapped[k] for k in sorted(swapped)]

    all_rows = pool * count
    chunks_in = [VMEM] * len(operands)
    shrink, slots, token = call(
        "shrink",
        functools.partial(shrink_kernel, pool, parts, count, half),
        (*operands, adapter_down_weight),
        chunks_in + [VMEM],
        [struct((all_rows, LANES), BF16), struct((all_rows, LANES), F32), TOKEN],
        work=2 * all_rows * part * down_here * LANES,
        moved=4 << 20,
    )
    weight, marked = lax.optimization_barrier((key_value_weight, token))
    rank = adapter_up_key.shape[1]
    base, table, token = call(
        "base",
        functools.partial(base_kernel, pool, parts, count, half),
        (*operands, jnp.transpose(weight, (1, 0, 2)), adapter_up_key, adapter_up_value, marked),
        chunks_in + [VMEM] * 3 + [ANY],
        [
            struct((all_rows, kv_local * pair), F32),
            struct((up_here * 2 * rank, kv_local * pair), BF16),
            TOKEN,
        ],
        work=2 * all_rows * part * kv_local * pair,
        moved=3 << 20,
    )

    ratio = pool // tensor
    mine = None
    for j in range(ratio):
        for m in range(parts - 1, tensor, parts):
            pairs = [
                (i * tensor + s, (s * ratio + ((i // tensor) ^ j)) * tensor + ((i % tensor) ^ m))
                for i in range(pool)
                for s in range(tensor)
            ]
            moved = lax.ppermute(shrink, ("pool", "tensor"), pairs).astype(F32)
            mine = moved if mine is None else mine + moved
    mine = mine + token[:1]
    sums = [mine] + ([over_pair(mine)] if parts == 2 else [])
    expanded = call(
        "expand",
        functools.partial(expand_kernel, pool, parts),
        (*sums, slots, base, table),
        [VMEM] * (parts + 3),
        [struct((count, kv_local * pair), F32)] + [struct((count, kv_local * pair), BF16)] * (pool - 1) + [TOKEN],
        [pltpu.VMEM((all_rows, LANES), F32), pltpu.VMEM((all_rows, kv_local * pair), F32)],
        work=4 * all_rows * LANES * up_here * LANES,
    )
    received = [None] * pool
    for k in range(pool - 1, 0, -1):
        received[k] = lax.ppermute(expanded[k], "pool", [(i, (i + k) % pool) for i in range(pool)])
    acc, top, total, bias = call(
        "cached",
        cache_kernel,
        (packed[-1], queries, stored, expanded[pool]),
        [VMEM] * 3 + [ANY],
        [struct((count * heads, n), F32) for n in (size, size, size, count * kv_local)],
        [pltpu.VMEM((count * heads, cache.shape[1]), t) for t in (F32, BF16)],
        work=4 * count * heads * cache.shape[1] * kv_local * size,
        moved=cache.size * 2,
    )
    return tuple(call(
        "finish",
        functools.partial(finish_kernel, pool),
        (expanded[0], *[received[k] for k in [*range(2, pool), 1]], queries, acc, top, total, bias),
        [VMEM] * (pool + 5),
        [struct((rows, steps_new, heads * size), BF16), struct((rows, steps_new, kv_local, pair), BF16)],
        [pltpu.VMEM((count * heads, size), F32)],
        work=4 * count * heads * size * LANES,
    ))


def solution(mesh):
    return jax.shard_map(
        body,
        mesh=mesh,
        in_specs=(
            P(("groups", "pool"), None, None),
            P(("groups", "pool"), None, "tensor", None),
            P(("groups", "pool"), None, "tensor", None),
            P("pool", "tensor", None),
            P("tensor", "pool", None),
            P("pool", None, "tensor", None),
            P("pool", None, "tensor", None),
            P(("groups", "pool")),
            P(),
            P(("groups", "pool")),
        ),
        out_specs=(
            P(("groups", "pool"), None, "tensor"),
            P(("groups", "pool"), None, "tensor", None),
        ),
        check_vma=False,
    )
```
